256 devices in a mesh: group: 2 (over core), dp: 64 (over x, y_lo, z), mp: 2 (over y_hi).
Axes of the slice: x: 4, y: 4 (y_hi: 2, y_lo: 2; y = y_hi * 2 + y_lo), z: 8, core: 2. Of those that a mesh axis runs over, the one named last changes fastest.
Arguments:
- attention_result: bfloat16 [131072, 2432], P(('group', 'dp'), 'mp'), may hold values from -6 to 6
- resid: bfloat16 [131072, 2432], P(('group', 'dp', 'mp')), may hold values from -6 to 6
- attention_output_weight: bfloat16 [2432, 2432], P('mp', 'dp'), may hold values from -0.125 to 0.125
- adapter_down: bfloat16 [2432, 64], P('mp'), may hold values from -0.125 to 0.125
- adapter_up: bfloat16 [64, 2432], replicated, may hold values from -0.75 to 0.75
- branch_gate: bfloat16 [2432], replicated, may hold values from 0.5 to 1.5
- final_norm_scale: bfloat16 [2432], replicated, may hold values from -1.5 to 1.5
- final_norm_shift: bfloat16 [2432], replicated, may hold values from -1.5 to 1.5
- velocity_weight: bfloat16 [2432, 64], replicated, may hold values from -0.125 to 0.125
- velocity_bias: bfloat16 [64], replicated, may hold values from -1.5 to 1.5
- noised_latent_tokens: bfloat16 [131072, 64], P(('group', 'dp', 'mp')), may hold values from -6 to 6
- decoder_weight: bfloat16 [64, 768], replicated, may hold values from -0.75 to 0.75
- decoder_bias: bfloat16 [768], replicated, may hold values from -1.5 to 1.5
- patch_embed_weight: bfloat16 [768, 1280], replicated, may hold values from -0.21875 to 0.21875
- reward_norm_gain: bfloat16 [1280], replicated, may hold values from 0.5 to 1.5
- reward_head_bank: bfloat16 [64, 1280, 1024], P('dp'), may hold values from -0.15625 to 0.15625
- prompt_features: bfloat16 [16384, 1024], P(('group', 'dp', 'mp')), may hold values from -6 to 6
- assignment: int32 [16384, 1], P(('group', 'dp', 'mp')), may hold values from 0 to 63; in each aligned block of 64 rows (0 to 63, 64 to 127, ...) at most 2 rows name the same one
Outputs:
- grad_a: float32 [2432, 64], P('mp')
- grad_b: float32 [64, 2432], replicated
- crop_scores: bfloat16 [16384], P(('group', 'dp', 'mp'))
The draws below stay inside these ranges and needn't reach their ends.
Inputs may be any that keep to these rules, and one draw needn't show every extreme that they name: `assignment`: row k names the reward head that scores crop k. Among the crops of one device (aligned blocks of 64 rows) no head is named more than 2 times, a bound that some block reaches.
All inputs are finite; a program needn't handle non-finite values.
Results may differ from the reference program's by a relative error of at most 0.02.
Values may be sent and summed in bfloat16 or wider, within the bound.
No kernel may reach another device: no remote copies, remote signals or barrier semaphores. Data moves between devices by JAX's collectives and lax.ppermute only.
A program may use at most 128 MiB of HBM per device.

```python
import math
import jax
import jax.numpy as jnp
import numpy as np
from jax import lax

MODEL_WIDTH = 2432
LAT = 64
PIX = 768
VW = 1280
EMB = 1024
ADAPTER_RANK = 64
TILE = 8
TILES_DEV = 64
CAP = 2
RHEADS = 64
TILES = 16384
TOKENS = 131072
N_DP = 64


def block_scale(rng, extent, cuts, smallest, largest):
    def one(position, blocks):
        heights = jax.random.uniform(jax.random.fold_in(jax.random.fold_in(rng, 6), position), (blocks,), jnp.float32, smallest / len(cuts), largest / len(cuts))
        return jnp.repeat(jnp.exp(heights), extent[position] // blocks).reshape((-1,) + (1,) * (len(extent) - position - 1))

    loudness = one(*cuts[0])
    for cut in cuts[1:]:
        loudness = loudness * one(*cut)
    return loudness


def routed_block(own_key, own, number, rows, number_of, top, limit, skew):
    ranking = jax.random.permutation(own_key, number_of)
    heavy_load, ordinary = portions_of(number_of, rows * top, limit, skew, True), portions_of(number_of, rows * top, limit, skew, False)
    places = jnp.arange(number_of)

    def named(lengths, offset_by):
        used = int((lengths > 0).sum())
        fixed = max(1, used // 4)
        shifted = fixed + (places - fixed + offset_by * (used - fixed)) % max(1, number_of - fixed)
        return jnp.zeros((number_of,), jnp.int32).at[ranking[jnp.where(places < fixed, places, shifted)]].set(jnp.asarray(lengths, jnp.int32))

    lengths = jnp.where(number % 4 == 0, named(heavy_load, number // 4), named(ordinary, number - number // 4 - 1))
    mixed = jax.random.permutation(jax.random.fold_in(own, 3), number_of)
    source_of, taker = mixed[0:number_of // 2 * 2:2], mixed[1:number_of // 2 * 2:2]
    margin = jnp.minimum(lengths[source_of] - 1, limit - lengths[taker]) // 2
    margin = jnp.where((source_of == ranking[0]) | (taker == ranking[0]) | (lengths[taker] == 0), 0, jnp.maximum(margin, 0))
    shifted = jax.random.randint(jax.random.fold_in(own, 4), (number_of // 2,), 0, 1 << 20) % (margin + 1)
    lengths = lengths.at[source_of].add(-shifted).at[taker].add(shifted)
    items = jnp.searchsorted(jnp.cumsum(lengths), jnp.arange(rows * top), side="right").astype(jnp.int32)
    grid = items.reshape(top, rows).T
    grid = grid[jax.random.permutation(jax.random.fold_in(own, 1), rows)]
    offset_by = jax.random.randint(jax.random.fold_in(own, 2), (rows, 1), 0, top)
    return jnp.take_along_axis(grid, (jnp.arange(top)[None, :] + offset_by) % top, axis=1)


def portions_of(amount, total, bound, skew, full):
    weights = [(1 << 20) // math.isqrt(grade ** skew) + 1 for grade in range(1, amount + 1)]
    largest = bound if full else min(bound, max(-(-total // amount), total * weights[0] // sum(weights)))
    least = 1 if total - largest >= amount - 1 else 0
    given, rest = [largest] + [least] * (amount - 1), total - largest - least * (amount - 1)
    while rest > 0:
        free = [i for i in range(1, amount) if given[i] < largest] or [i for i in range(1, amount) if given[i] < bound]
        mass, remaining = sum([weights[i] for i in free]), rest
        for i in free:
            addition = min(bound - given[i], max(1, remaining * weights[i] // mass), rest)
            given[i] = given[i] + addition
            rest = rest - addition
    return np.array(given)


def gaussian(stream_key, extent, scale, bound, pieces=(), kind=jnp.bfloat16):
    array = jax.random.normal(stream_key, extent, jnp.float32) * scale
    if len(pieces) > 0:
        array = block_scale(stream_key, extent, pieces, -0.22, 0.18) * array
    return jnp.clip(array, min=-bound, max=bound).astype(kind)


def setup_inputs(seed: int = 0) -> dict:
    seeds = jax.random.split(jax.random.key(seed), 19)
    attention_result = gaussian(seeds[0], (TOKENS, MODEL_WIDTH), 1.0, 6.0, ((0, 128), (1, 2)))
    resid = gaussian(seeds[1], (TOKENS, MODEL_WIDTH), 1.0, 6.0, ((0, 256),))
    attention_output_weight = gaussian(seeds[2], (MODEL_WIDTH, MODEL_WIDTH), MODEL_WIDTH ** -0.5, 0.125, ((0, 2), (1, 64)))
    adapter_down = gaussian(seeds[3], (MODEL_WIDTH, ADAPTER_RANK), MODEL_WIDTH ** -0.5, 0.125, ((0, 2),))
    adapter_up = gaussian(seeds[4], (ADAPTER_RANK, MODEL_WIDTH), ADAPTER_RANK ** -0.5, 0.75)
    branch_gate = jnp.clip(1.0 + 0.1 * jax.random.normal(seeds[5], (MODEL_WIDTH,), jnp.float32), 0.5, 1.5).astype(jnp.bfloat16)
    final_norm_scale = gaussian(seeds[6], (MODEL_WIDTH,), 0.3, 1.5)
    final_norm_shift = gaussian(seeds[7], (MODEL_WIDTH,), 0.3, 1.5)
    velocity_weight = gaussian(seeds[8], (MODEL_WIDTH, LAT), MODEL_WIDTH ** -0.5, 0.125)
    velocity_bias = gaussian(seeds[9], (LAT,), 0.3, 1.5)
    noised_latent_tokens = gaussian(seeds[10], (TOKENS, LAT), 1.0, 6.0, ((0, 256),))
    decoder_weight = gaussian(seeds[11], (LAT, PIX), LAT ** -0.5, 0.75)
    decoder_bias = gaussian(seeds[12], (PIX,), 0.3, 1.5)
    patch_embed_weight = gaussian(seeds[13], (PIX, VW), PIX ** -0.5, 0.21875)
    reward_norm_gain = jnp.clip(1.0 + 0.1 * jax.random.normal(seeds[14], (VW,), jnp.float32), 0.5, 1.5).astype(jnp.bfloat16)
    reward_head_bank = gaussian(seeds[15], (RHEADS, VW, EMB), VW ** -0.5, 0.15625, ((0, 64),))
    prompt_features = gaussian(seeds[16], (TILES, EMB), 1.0, 6.0, ((0, 256),))
    assignment_keys = jax.random.split(jax.random.fold_in(seeds[17], 1), TILES // TILES_DEV)
    assignment_turns = jax.random.permutation(jax.random.fold_in(seeds[17], 3), TILES // TILES_DEV)
    assignment = jax.vmap(lambda own, number: routed_block(jax.random.fold_in(seeds[17], 2), own, number, TILES_DEV, N_DP, 1, CAP, 2))(assignment_keys, assignment_turns).reshape((TILES, 1))
    return dict(attention_result=attention_result, resid=resid, attention_output_weight=attention_output_weight, adapter_down=adapter_down, adapter_up=adapter_up, branch_gate=branch_gate, final_norm_scale=final_norm_scale, final_norm_shift=final_norm_shift, velocity_weight=velocity_weight, velocity_bias=velocity_bias, noised_latent_tokens=noised_latent_tokens, decoder_weight=decoder_weight, decoder_bias=decoder_bias, patch_embed_weight=patch_embed_weight, reward_norm_gain=reward_norm_gain, reward_head_bank=reward_head_bank, prompt_features=prompt_features, assignment=assignment)


epsilon = 1e-06
sigma_last = 0.7
loss_weight = 16.0

def product_final(left, right):
    return lax.dot_general(left, right, (((1,), (1,)), ((), ())), preferred_element_type=jnp.float32)

def dot_first(left, right):
    return lax.dot_general(left, right, (((0,), (0,)), ((), ())), preferred_element_type=jnp.float32)

def normalize(values):
    centre = values - lax.optimization_barrier(jnp.mean(values, -1, keepdims=True))
    inverse_std = lax.rsqrt(lax.optimization_barrier(jnp.mean(centre * centre, -1, keepdims=True)) + epsilon)
    return (centre * inverse_std, inverse_std)

def norm_back(grad_normed, normed, inverse_std):
    grad_mean = lax.optimization_barrier(jnp.mean(grad_normed, -1, keepdims=True))
    cross_mean = lax.optimization_barrier(jnp.mean(grad_normed * normed, -1, keepdims=True))
    return (grad_normed - grad_mean - normed * cross_mean) * inverse_std

def tail_forward(projected_rows, resid, branch_gate, final_norm_scale, final_norm_shift, velocity_weight, velocity_bias, noised_latent_tokens, decoder_weight, decoder_bias):
    stream = resid.astype(jnp.float32) + branch_gate.astype(jnp.float32) * projected_rows
    normed, inverse_std = normalize(stream)
    modulated = (normed * (1.0 + final_norm_scale.astype(jnp.float32)) + final_norm_shift.astype(jnp.float32)).astype(jnp.bfloat16)
    velocity = jnp.dot(modulated, velocity_weight, preferred_element_type=jnp.float32) + velocity_bias.astype(jnp.float32)
    latent = noised_latent_tokens.astype(jnp.float32) - sigma_last * velocity
    inner = jnp.dot(latent.astype(jnp.bfloat16), decoder_weight, preferred_element_type=jnp.float32) + decoder_bias.astype(jnp.float32)
    return (jnp.tanh(inner), normed, inverse_std)

def tail_backward(pixel_grad, decoded, normed, inverse_std, branch_gate, final_norm_scale, velocity_weight, decoder_weight):
    grad_inner = (pixel_grad.astype(jnp.float32) * (1.0 - decoded * decoded)).astype(jnp.bfloat16)
    grad_latent = product_final(grad_inner, decoder_weight)
    grad_velocity = (-sigma_last * grad_latent).astype(jnp.bfloat16)
    grad_modulated = product_final(grad_velocity, velocity_weight)
    grad_stream = norm_back(grad_modulated * (1.0 + final_norm_scale.astype(jnp.float32)), normed, inverse_std)
    return (branch_gate.astype(jnp.float32) * grad_stream).astype(jnp.bfloat16)

def crop_embed(pixels, patch_embed_weight, reward_norm_gain):
    count, tile_len, width = pixels.shape
    embedded = jnp.dot(pixels.reshape(count * tile_len, width), patch_embed_weight, preferred_element_type=jnp.float32)
    normed, inverse_std = normalize(embedded)
    scaled = (normed * reward_norm_gain.astype(jnp.float32)).reshape(count, tile_len, embedded.shape[1])
    return (lax.optimization_barrier(jnp.mean(scaled, 1)).astype(jnp.bfloat16), normed, inverse_std)

def crop_score(query, text):
    text_wide = text.astype(jnp.float32)
    width = query.shape[-1]
    query_rms = jnp.sqrt(lax.optimization_barrier(jnp.mean(query * query, -1, keepdims=True)) + epsilon)
    text_rms = jnp.sqrt(lax.optimization_barrier(jnp.mean(text_wide * text_wide, -1, keepdims=True)) + epsilon)
    scores = lax.optimization_barrier(jnp.mean(query * text_wide, -1, keepdims=True)) / (query_rms * text_rms)
    grad_query = -loss_weight * (text_wide / (width * query_rms * text_rms) - scores * query / (width * query_rms * query_rms))
    return (scores[:, 0], grad_query.astype(jnp.bfloat16))

def crop_back(grad_pooled, normed, inverse_std, reward_norm_gain, patch_embed_weight, tile_len):
    count, width = grad_pooled.shape
    spread = jnp.broadcast_to((grad_pooled / tile_len)[:, None, :], (count, tile_len, width)).reshape(count * tile_len, width)
    grad_embedded = norm_back(spread * reward_norm_gain.astype(jnp.float32), normed, inverse_std).astype(jnp.bfloat16)
    return product_final(grad_embedded, patch_embed_weight).astype(jnp.bfloat16)

def head_apply(rows, heads, assignment, backward):
    count = rows.shape[0]
    head_of = assignment[:, 0].astype(jnp.int32)
    bound_rows = min(count, count // TILES_DEV * CAP)
    sort_order = jnp.argsort(head_of, stable=True).astype(jnp.int32)
    counts = lax.optimization_barrier(jnp.sum((head_of[:, None] == jnp.arange(RHEADS, dtype=jnp.int32)[None, :]).astype(jnp.int32), 0))
    starts = (jnp.cumsum(counts) - counts).astype(jnp.int32)
    ordered = jnp.concatenate([rows[sort_order], jnp.zeros((bound_rows, rows.shape[1]), rows.dtype)], 0)
    width = heads.shape[1] if backward else heads.shape[2]

    def advance(carry, head_index):
        block = lax.dynamic_slice_in_dim(ordered, starts[head_index], bound_rows, 0)
        weights = heads[head_index]
        result = product_final(block, weights) if backward else jnp.dot(block, weights, preferred_element_type=jnp.float32)
        return (lax.dynamic_update_slice_in_dim(carry, result, starts[head_index], 0), None)
    filled, _ = lax.scan(advance, jnp.zeros((count + bound_rows, width), jnp.float32), jnp.arange(RHEADS, dtype=jnp.int32))
    inverse = jnp.argsort(sort_order).astype(jnp.int32)
    return filled[:count][inverse]

def reference(attention_result, resid, attention_output_weight, adapter_down, adapter_up, branch_gate, final_norm_scale, final_norm_shift, velocity_weight, velocity_bias, noised_latent_tokens, decoder_weight, decoder_bias, patch_embed_weight, reward_norm_gain, reward_head_bank, prompt_features, assignment):
    block_rows = math.gcd(TOKENS, 8192)
    blocks = TOKENS // block_rows
    adapter_widened = adapter_up.astype(jnp.float32)

    def generator_rows(index):
        start = index * block_rows
        input_arrays = lax.dynamic_slice_in_dim(attention_result, start, block_rows, 0)
        lowrank_adapter = jnp.dot(input_arrays, adapter_down, preferred_element_type=jnp.float32)
        projected_rows = jnp.dot(input_arrays, attention_output_weight, preferred_element_type=jnp.float32) + jnp.dot(lowrank_adapter, adapter_widened, precision=lax.Precision.HIGHEST)
        decoded, normed, inverse_std = tail_forward(projected_rows, lax.dynamic_slice_in_dim(resid, start, block_rows, 0), branch_gate, final_norm_scale, final_norm_shift, velocity_weight, velocity_bias, lax.dynamic_slice_in_dim(noised_latent_tokens, start, block_rows, 0), decoder_weight, decoder_bias)
        return (input_arrays, lowrank_adapter, decoded, normed, inverse_std)

    def forward_block(index):
        return generator_rows(index)[2].astype(jnp.bfloat16)
    pixels = lax.map(forward_block, jnp.arange(blocks, dtype=jnp.int32)).reshape(TILES, TILE, PIX)
    pooled, crop_normed, crop_inverse = crop_embed(pixels, patch_embed_weight, reward_norm_gain)
    query = head_apply(pooled, reward_head_bank, assignment, False)
    scores, grad_query = crop_score(query, prompt_features)
    grad_pooled = head_apply(grad_query, reward_head_bank, assignment, True)
    pixel_grad = crop_back(grad_pooled, crop_normed, crop_inverse, reward_norm_gain, patch_embed_weight, TILE).reshape(TOKENS, PIX)

    def backward_block(totals, index):
        input_arrays, lowrank_adapter, decoded, normed, inverse_std = generator_rows(index)
        grads = lax.dynamic_slice_in_dim(pixel_grad, index * block_rows, block_rows, 0)
        output_gradient = tail_backward(grads, decoded, normed, inverse_std, branch_gate, final_norm_scale, velocity_weight, decoder_weight)
        rank_gradient = product_final(output_gradient, adapter_up).astype(jnp.bfloat16)
        return ((totals[0] + dot_first(input_arrays, rank_gradient), totals[1] + dot_first(lowrank_adapter.astype(jnp.bfloat16), output_gradient)), None)
    start_totals = (jnp.zeros((MODEL_WIDTH, ADAPTER_RANK), jnp.float32), jnp.zeros((ADAPTER_RANK, MODEL_WIDTH), jnp.float32))
    (grad_a, grad_b), _ = lax.scan(backward_block, start_totals, jnp.arange(blocks, dtype=jnp.int32))
    return (grad_a, grad_b, scores.astype(jnp.bfloat16))
```

```python
import jax
import jax.numpy as jnp
from jax import lax
from jax.sharding import Mesh
from jax.sharding import PartitionSpec as P

TILE = 8


epsilon = 1e-06
sigma_last = 0.7
loss_weight = 16.0


def product_final(left, right):
    return lax.dot_general(
        left, right, (((1,), (1,)), ((), ())), preferred_element_type=jnp.float32
    )


def dot_first(left, right):
    return lax.dot_general(
        left, right, (((0,), (0,)), ((), ())), preferred_element_type=jnp.float32
    )


def normalize(values):
    centre = values - jnp.mean(values, -1, keepdims=True)
    inverse_std = lax.rsqrt(jnp.mean(centre * centre, -1, keepdims=True) + epsilon)
    return (centre * inverse_std, inverse_std)


def norm_back(grad_normed, normed, inverse_std):
    grad_mean = jnp.mean(grad_normed, -1, keepdims=True)
    cross_mean = jnp.mean(grad_normed * normed, -1, keepdims=True)
    return (grad_normed - grad_mean - normed * cross_mean) * inverse_std


def tail_forward(
    projected_rows,
    resid,
    branch_gate,
    final_norm_scale,
    final_norm_shift,
    velocity_weight,
    velocity_bias,
    noised_latent_tokens,
    decoder_weight,
    decoder_bias,
):
    stream = resid.astype(jnp.float32) + branch_gate.astype(jnp.float32) * projected_rows
    normed, inverse_std = normalize(stream)
    modulated = (
        normed * (1.0 + final_norm_scale.astype(jnp.float32)) + final_norm_shift.astype(jnp.float32)
    ).astype(jnp.bfloat16)
    velocity = jnp.dot(
        modulated, velocity_weight, preferred_element_type=jnp.float32
    ) + velocity_bias.astype(jnp.float32)
    latent = noised_latent_tokens.astype(jnp.float32) - sigma_last * velocity
    inner = jnp.dot(
        latent.astype(jnp.bfloat16), decoder_weight, preferred_element_type=jnp.float32
    ) + decoder_bias.astype(jnp.float32)
    return (jnp.tanh(inner), normed, inverse_std)


def tail_backward(
    pixel_grad,
    decoded,
    normed,
    inverse_std,
    branch_gate,
    final_norm_scale,
    velocity_weight,
    decoder_weight,
):
    grad_inner = (pixel_grad.astype(jnp.float32) * (1.0 - decoded * decoded)).astype(jnp.bfloat16)
    grad_latent = product_final(grad_inner, decoder_weight)
    grad_velocity = (-sigma_last * grad_latent).astype(jnp.bfloat16)
    grad_modulated = product_final(grad_velocity, velocity_weight)
    grad_stream = norm_back(
        grad_modulated * (1.0 + final_norm_scale.astype(jnp.float32)), normed, inverse_std
    )
    return (branch_gate.astype(jnp.float32) * grad_stream).astype(jnp.bfloat16)


def crop_embed(pixels, patch_embed_weight, reward_norm_gain):
    count, tile_len, width = pixels.shape
    embedded = jnp.dot(
        pixels.reshape(count * tile_len, width),
        patch_embed_weight,
        preferred_element_type=jnp.float32,
    )
    normed, inverse_std = normalize(embedded)
    scaled = (normed * reward_norm_gain.astype(jnp.float32)).reshape(
        count, tile_len, embedded.shape[1]
    )
    return (jnp.mean(scaled, 1).astype(jnp.bfloat16), normed, inverse_std)


def crop_score(query, text):
    text_wide = text.astype(jnp.float32)
    width = query.shape[-1]
    query_rms = jnp.sqrt(jnp.mean(query * query, -1, keepdims=True) + epsilon)
    text_rms = jnp.sqrt(jnp.mean(text_wide * text_wide, -1, keepdims=True) + epsilon)
    scores = jnp.mean(query * text_wide, -1, keepdims=True) / (query_rms * text_rms)
    grad_query = -loss_weight * (
        text_wide / (width * query_rms * text_rms)
        - scores * query / (width * query_rms * query_rms)
    )
    return (scores[:, 0], grad_query.astype(jnp.bfloat16))


def crop_back(grad_pooled, normed, inverse_std, reward_norm_gain, patch_embed_weight, tile_len):
    count, width = grad_pooled.shape
    spread = jnp.broadcast_to(
        (grad_pooled / tile_len)[:, None, :], (count, tile_len, width)
    ).reshape(count * tile_len, width)
    grad_embedded = norm_back(
        spread * reward_norm_gain.astype(jnp.float32), normed, inverse_std
    ).astype(jnp.bfloat16)
    return product_final(grad_embedded, patch_embed_weight).astype(jnp.bfloat16)


CHIPS = ("x", "yl", "z", "mp")
DP = ("x", "yl", "z")


def shift(block, axis, size, step):
    return lax.ppermute(block, axis, [(i, (i + step) % size) for i in range(size)])


def ring(block, axis, size):
    held = [(0, block)]
    up = down = block
    for step in range(1, size // 2):
        up, down = shift(up, axis, size, 1), shift(down, axis, size, -1)
        held += [(-step, up), (step, down)]
    half = block.shape[0] // 2
    if half == 0 or block.shape[0] % 2:
        held.append((size // 2, shift(up, axis, size, 1)))
    else:
        first = shift(up[:half], axis, size, 1)
        second = shift(down[half:], axis, size, -1)
        held.append((size // 2, jnp.concatenate([first, second], 0)))
    return held


def place(blocks, axis, size):
    own = lax.axis_index(axis)
    shape = blocks[0][1].shape
    filled = jnp.zeros((size,) + shape, blocks[0][1].dtype)
    for offset, block in blocks:
        filled = lax.dynamic_update_index_in_dim(filled, block, (own + offset + size) % size, 0)
    return filled


def swap_cores(block):
    return lax.ppermute(block, "group", [(0, 1), (1, 0)])


def gather_weight(shard):
    picked = lax.ppermute(shard, ("group", "mp"), [(0, 0), (2, 1), (1, 2), (3, 3)])
    beside = shift(picked, "yl", 2, 1)
    pair = jnp.where(
        lax.axis_index("yl") == 0, jnp.stack([picked, beside]), jnp.stack([beside, picked])
    )
    columns, width = shard.shape
    along_z = place(ring(pair, "z", 8), "z", 8)
    block = jnp.transpose(along_z, (1, 0, 2, 3)).reshape(16 * columns, width)
    own = ring(block, "x", 4)
    other = [(offset, swap_cores(part)) for offset, part in own]
    return (
        place(own, "x", 4).reshape(64 * columns, width),
        place(other, "x", 4).reshape(64 * columns, width),
    )


def shards(
    attention_result,
    resid,
    attention_output_weight,
    adapter_down,
    adapter_up,
    branch_gate,
    final_norm_scale,
    final_norm_shift,
    velocity_weight,
    velocity_bias,
    noised_latent_tokens,
    decoder_weight,
    decoder_bias,
    patch_embed_weight,
    reward_norm_gain,
    reward_head_bank,
    prompt_features,
    assignment,
):
    group, mp = lax.axis_index("group"), lax.axis_index("mp")
    row_count, width = resid.shape
    half = width // 2
    tiles_dev = row_count // TILE
    weight_own, weight_other = gather_weight(attention_output_weight.T)
    kept = lax.dynamic_slice_in_dim(attention_result, mp * row_count, row_count, 0)
    given = lax.dynamic_slice_in_dim(attention_result, (1 - mp) * row_count, row_count, 0)
    taken = shift(given, "mp", 2, 1)
    down_other = shift(adapter_down, "mp", 2, 1)

    dp_count = 64
    capacity = 2
    target = assignment[:, 0]
    earlier = jnp.arange(tiles_dev)[None, :] < jnp.arange(tiles_dev)[:, None]
    matches = jnp.logical_and(target[:, None] == target[None, :], earlier)
    slot_index = jnp.sum(matches.astype(jnp.int32), 1)
    position = target * capacity + slot_index
    select = (
        jnp.arange(dp_count * capacity, dtype=jnp.int32)[:, None] == position[None, :]
    ).astype(jnp.bfloat16)
    texts = jnp.dot(select, prompt_features, preferred_element_type=jnp.float32)
    texts = texts.astype(jnp.bfloat16).reshape(dp_count, capacity, prompt_features.shape[1])
    crop_texts = lax.all_to_all(texts, DP, split_axis=0, concat_axis=0, tiled=True)

    same = group == mp
    for_own = jnp.where(same, kept, taken)
    for_other = jnp.where(same, taken, kept)
    lowrank_adapter = jnp.dot(kept, adapter_down, preferred_element_type=jnp.float32) + jnp.dot(
        taken, down_other, preferred_element_type=jnp.float32
    )
    projected_rows = (
        product_final(for_own, weight_own)
        + product_final(for_other, weight_other)
        + jnp.dot(
            lowrank_adapter, adapter_up.astype(jnp.float32), precision=lax.Precision.HIGHEST
        )
    )
    decoded, normed, inverse_std = tail_forward(
        projected_rows,
        resid,
        branch_gate,
        final_norm_scale,
        final_norm_shift,
        velocity_weight,
        velocity_bias,
        noised_latent_tokens,
        decoder_weight,
        decoder_bias,
    )
    pixels = decoded.astype(jnp.bfloat16)
    width_pix = pixels.shape[1]
    pooled, crop_normed, crop_inverse = crop_embed(
        pixels.reshape(tiles_dev, TILE, width_pix), patch_embed_weight, reward_norm_gain
    )
    width_view = pooled.shape[1]
    packed = jnp.dot(select, pooled, preferred_element_type=jnp.float32).astype(jnp.bfloat16)
    own_head = reward_head_bank[0]
    crop_pooled = lax.all_to_all(
        packed.reshape(dp_count, capacity, width_view), DP, split_axis=0, concat_axis=0, tiled=True
    ).reshape(dp_count * capacity, width_view)
    query = jnp.dot(crop_pooled, own_head, preferred_element_type=jnp.float32)
    scores, grad_query = crop_score(query, crop_texts.reshape(dp_count * capacity, -1))
    grad_pooled = product_final(grad_query, own_head).astype(jnp.bfloat16)
    back = jnp.concatenate(
        [grad_pooled, jnp.broadcast_to(scores.astype(jnp.bfloat16)[:, None], (dp_count * capacity, 128))],
        1,
    )
    back = lax.all_to_all(
        back.reshape(dp_count, capacity, width_view + 128), DP, split_axis=0, concat_axis=0, tiled=True
    ).reshape(dp_count * capacity, width_view + 128)
    back = dot_first(select, back)
    own_scores = back[:, width_view].astype(jnp.bfloat16)
    pixel_grad = crop_back(
        back[:, :width_view], crop_normed, crop_inverse, reward_norm_gain, patch_embed_weight, TILE
    )
    output_gradient = tail_backward(
        pixel_grad,
        decoded,
        normed,
        inverse_std,
        branch_gate,
        final_norm_scale,
        velocity_weight,
        decoder_weight,
    )
    rank_grad = product_final(output_gradient, adapter_up).astype(jnp.bfloat16)
    grad_b = dot_first(lowrank_adapter.astype(jnp.bfloat16), output_gradient)
    grad_b = jnp.concatenate([grad_b[:, :half], grad_b[:, half:]], 0)
    first = mp == 0
    grad_kept, grad_taken = dot_first(rank_grad, kept), dot_first(rank_grad, taken)
    grad_a = jnp.concatenate(
        [jnp.where(first, grad_kept, grad_taken), jnp.where(first, grad_taken, grad_kept)], 0
    )
    lead = group == 0
    mine = jnp.where(lead, grad_a, grad_b)
    given_part = jnp.where(lead, grad_b, grad_a).astype(jnp.bfloat16)
    mine = mine + swap_cores(given_part).astype(jnp.float32)
    parts = lax.all_to_all(
        mine.astype(jnp.bfloat16), CHIPS, split_axis=0, concat_axis=0, tiled=True
    )
    total = jnp.sum(parts.astype(jnp.float32), 0, keepdims=True).astype(jnp.bfloat16)
    total = lax.all_to_all(
        jnp.broadcast_to(total, parts.shape), CHIPS, split_axis=0, concat_axis=0, tiled=True
    )
    passed = swap_cores(total)
    total_a = jnp.where(lead, total, passed)
    total_b = jnp.where(lead, passed, total)
    rank = adapter_up.shape[0]
    grad_a = lax.dynamic_slice_in_dim(total_a, mp * rank, rank, 0).astype(jnp.float32).T
    grad_b = jnp.concatenate([total_b[:rank], total_b[rank:]], 1).astype(jnp.float32)
    return (grad_a, grad_b, own_scores)


def solution(mesh):
    fine = Mesh(mesh.devices.reshape(2, 4, 2, 8, 2), ("group", "x", "yl", "z", "mp"))
    dp = ("x", "yl", "z")
    rows = ("group",) + dp
    return jax.shard_map(
        shards,
        mesh=fine,
        in_specs=(
            P(rows, "mp"),
            P(rows + ("mp",), None),
            P("mp", dp),
            P("mp", None),
            P(),
            P(),
            P(),
            P(),
            P(),
            P(),
            P(rows + ("mp",), None),
            P(),
            P(),
            P(),
            P(),
            P(dp, None, None),
            P(rows + ("mp",), None),
            P(rows + ("mp",), None),
        ),
        out_specs=(P("mp", None), P(), P(rows + ("mp",))),
        check_vma=False,
    )
```

```python
import jax
import jax.numpy as jnp
from jax import lax
from jax.sharding import Mesh
from jax.sharding import PartitionSpec as P

TILE = 8


epsilon = 1e-06
sigma_last = 0.7
loss_weight = 16.0


def product_final(left, right):
    return lax.dot_general(
        left, right, (((1,), (1,)), ((), ())), preferred_element_type=jnp.float32
    )


def dot_first(left, right):
    return lax.dot_general(
        left, right, (((0,), (0,)), ((), ())), preferred_element_type=jnp.float32
    )


def normalize(values):
    centre = values - jnp.mean(values, -1, keepdims=True)
    inverse_std = lax.rsqrt(jnp.mean(centre * centre, -1, keepdims=True) + epsilon)
    return (centre * inverse_std, inverse_std)


def norm_back(grad_normed, normed, inverse_std):
    grad_mean = jnp.mean(grad_normed, -1, keepdims=True)
    cross_mean = jnp.mean(grad_normed * normed, -1, keepdims=True)
    return (grad_normed - grad_mean - normed * cross_mean) * inverse_std


def tail_forward(
    projected_rows,
    resid,
    branch_gate,
    final_norm_scale,
    final_norm_shift,
    velocity_weight,
    velocity_bias,
    noised_latent_tokens,
    decoder_weight,
    decoder_bias,
):
    stream = resid.astype(jnp.float32) + branch_gate.astype(jnp.float32) * projected_rows
    normed, inverse_std = normalize(stream)
    modulated = (
        normed * (1.0 + final_norm_scale.astype(jnp.float32)) + final_norm_shift.astype(jnp.float32)
    ).astype(jnp.bfloat16)
    velocity = jnp.dot(
        modulated, velocity_weight, preferred_element_type=jnp.float32
    ) + velocity_bias.astype(jnp.float32)
    latent = noised_latent_tokens.astype(jnp.float32) - sigma_last * velocity
    inner = jnp.dot(
        latent.astype(jnp.bfloat16), decoder_weight, preferred_element_type=jnp.float32
    ) + decoder_bias.astype(jnp.float32)
    return (jnp.tanh(inner), normed, inverse_std)


def tail_backward(
    pixel_grad,
    decoded,
    normed,
    inverse_std,
    branch_gate,
    final_norm_scale,
    velocity_weight,
    decoder_weight,
):
    grad_inner = (pixel_grad.astype(jnp.float32) * (1.0 - decoded * decoded)).astype(jnp.bfloat16)
    grad_latent = product_final(grad_inner, decoder_weight)
    grad_velocity = (-sigma_last * grad_latent).astype(jnp.bfloat16)
    grad_modulated = product_final(grad_velocity, velocity_weight)
    grad_stream = norm_back(
        grad_modulated * (1.0 + final_norm_scale.astype(jnp.float32)), normed, inverse_std
    )
    return (branch_gate.astype(jnp.float32) * grad_stream).astype(jnp.bfloat16)


def crop_embed(pixels, patch_embed_weight, reward_norm_gain):
    count, tile_len, width = pixels.shape
    embedded = jnp.dot(
        pixels.reshape(count * tile_len, width),
        patch_embed_weight,
        preferred_element_type=jnp.float32,
    )
    normed, inverse_std = normalize(embedded)
    scaled = (normed * reward_norm_gain.astype(jnp.float32)).reshape(
        count, tile_len, embedded.shape[1]
    )
    return (jnp.mean(scaled, 1).astype(jnp.bfloat16), normed, inverse_std)


def crop_score(query, text):
    text_wide = text.astype(jnp.float32)
    width = query.shape[-1]
    query_rms = jnp.sqrt(jnp.mean(query * query, -1, keepdims=True) + epsilon)
    text_rms = jnp.sqrt(jnp.mean(text_wide * text_wide, -1, keepdims=True) + epsilon)
    scores = jnp.mean(query * text_wide, -1, keepdims=True) / (query_rms * text_rms)
    grad_query = -loss_weight * (
        text_wide / (width * query_rms * text_rms)
        - scores * query / (width * query_rms * query_rms)
    )
    return (scores[:, 0], grad_query.astype(jnp.bfloat16))


def crop_back(grad_pooled, normed, inverse_std, reward_norm_gain, patch_embed_weight, tile_len):
    count, width = grad_pooled.shape
    spread = jnp.broadcast_to(
        (grad_pooled / tile_len)[:, None, :], (count, tile_len, width)
    ).reshape(count * tile_len, width)
    grad_embedded = norm_back(
        spread * reward_norm_gain.astype(jnp.float32), normed, inverse_std
    ).astype(jnp.bfloat16)
    return product_final(grad_embedded, patch_embed_weight).astype(jnp.bfloat16)


CHIPS = ("x", "yl", "z", "mp")
DP = ("x", "yl", "z")


def shift(block, axis, size, step):
    return lax.ppermute(block, axis, [(i, (i + step) % size) for i in range(size)])


def ring(block, axis, size):
    held = [(0, block)]
    up = down = block
    for step in range(1, size // 2):
        up, down = shift(up, axis, size, 1), shift(down, axis, size, -1)
        held += [(-step, up), (step, down)]
    half = block.shape[0] // 2
    if half == 0 or block.shape[0] % 2:
        held.append((size // 2, shift(up, axis, size, 1)))
    else:
        first = shift(up[:half], axis, size, 1)
        second = shift(down[half:], axis, size, -1)
        held.append((size // 2, jnp.concatenate([first, second], 0)))
    return held


def lay_rows(blocks, rows, size):
    filled = jnp.zeros((size, blocks[0][1].shape[1]), blocks[0][1].dtype)
    for first, block in zip(rows, blocks):
        filled = lax.dynamic_update_slice_in_dim(filled, block[1], first, 0)
    return filled


def place(blocks, axis, size):
    own = lax.axis_index(axis)
    shape = blocks[0][1].shape
    filled = jnp.zeros((size,) + shape, blocks[0][1].dtype)
    for offset, block in blocks:
        filled = lax.dynamic_update_index_in_dim(filled, block, (own + offset + size) % size, 0)
    return filled


def swap_cores(block):
    return lax.ppermute(block, "group", [(0, 1), (1, 0)])


def gather_weight(shard):
    picked = lax.ppermute(shard, ("group", "mp"), [(0, 0), (2, 1), (1, 2), (3, 3)])
    beside = shift(picked, "yl", 2, 1)
    pair = jnp.where(
        lax.axis_index("yl") == 0, jnp.stack([picked, beside]), jnp.stack([beside, picked])
    )
    columns, width = shard.shape
    along_z = place(ring(pair, "z", 8), "z", 8)
    block = jnp.transpose(along_z, (1, 0, 2, 3)).reshape(16 * columns, width)
    up, down = shift(block, "x", 4, 1), shift(block, "x", 4, -1)
    half = block.shape[0] // 2
    first = shift(up[:half], "x", 4, 1)
    second = shift(down[half:], "x", 4, -1)
    held = [(0, block), (-1, up), (1, down), (2, first), (2, second)]
    own = lax.axis_index("x")
    rows = [((own + offset + 4) % 4) * block.shape[0] for offset, _ in held]
    rows[-1] = rows[-1] + half
    other = [(offset, swap_cores(part)) for offset, part in held]
    size = 64 * columns
    return lay_rows(held, rows, size), lay_rows(other, rows, size), block


def shards(
    attention_result,
    resid,
    attention_output_weight,
    adapter_down,
    adapter_up,
    branch_gate,
    final_norm_scale,
    final_norm_shift,
    velocity_weight,
    velocity_bias,
    noised_latent_tokens,
    decoder_weight,
    decoder_bias,
    patch_embed_weight,
    reward_norm_gain,
    reward_head_bank,
    prompt_features,
    assignment,
):
    group, mp = lax.axis_index("group"), lax.axis_index("mp")
    row_count, width = resid.shape
    half = width // 2
    tiles_dev = row_count // TILE
    weight_own, weight_other, block = gather_weight(attention_output_weight.T)
    sent, down_sent, texts_sent, _ = lax.optimization_barrier(
        (attention_result, adapter_down, prompt_features, block)
    )
    kept = lax.dynamic_slice_in_dim(attention_result, mp * row_count, row_count, 0)
    given = lax.dynamic_slice_in_dim(sent, (1 - mp) * row_count, row_count, 0)
    taken = shift(given, "mp", 2, 1)
    down_other = shift(down_sent, "mp", 2, 1)

    dp_count = 64
    capacity = 2
    target = assignment[:, 0]
    earlier = jnp.arange(tiles_dev)[None, :] < jnp.arange(tiles_dev)[:, None]
    matches = jnp.logical_and(target[:, None] == target[None, :], earlier)
    slot_index = jnp.sum(matches.astype(jnp.int32), 1)
    position = target * capacity + slot_index
    select = (
        jnp.arange(dp_count * capacity, dtype=jnp.int32)[:, None] == position[None, :]
    ).astype(jnp.bfloat16)
    texts = jnp.dot(select, texts_sent, preferred_element_type=jnp.float32)
    texts = texts.astype(jnp.bfloat16).reshape(dp_count, capacity, prompt_features.shape[1])
    crop_texts = lax.all_to_all(texts, DP, split_axis=0, concat_axis=0, tiled=True)

    same = group == mp
    for_own = jnp.where(same, kept, taken)
    for_other = jnp.where(same, taken, kept)
    lowrank_adapter = jnp.dot(kept, adapter_down, preferred_element_type=jnp.float32) + jnp.dot(
        taken, down_other, preferred_element_type=jnp.float32
    )
    projected_rows = (
        product_final(for_own, weight_own)
        + product_final(for_other, weight_other)
        + jnp.dot(
            lowrank_adapter, adapter_up.astype(jnp.float32), precision=lax.Precision.HIGHEST
        )
    )
    decoded, normed, inverse_std = tail_forward(
        projected_rows,
        resid,
        branch_gate,
        final_norm_scale,
        final_norm_shift,
        velocity_weight,
        velocity_bias,
        noised_latent_tokens,
        decoder_weight,
        decoder_bias,
    )
    pixels = decoded.astype(jnp.bfloat16)
    width_pix = pixels.shape[1]
    pooled, crop_normed, crop_inverse = crop_embed(
        pixels.reshape(tiles_dev, TILE, width_pix), patch_embed_weight, reward_norm_gain
    )
    width_view = pooled.shape[1]
    packed = jnp.dot(select, pooled, preferred_element_type=jnp.float32).astype(jnp.bfloat16)
    own_head = reward_head_bank[0]
    crop_pooled = lax.all_to_all(
        packed.reshape(dp_count, capacity, width_view), DP, split_axis=0, concat_axis=0, tiled=True
    ).reshape(dp_count * capacity, width_view)
    query = jnp.dot(crop_pooled, own_head, preferred_element_type=jnp.float32)
    scores, grad_query = crop_score(query, crop_texts.reshape(dp_count * capacity, -1))
    grad_pooled = product_final(grad_query, own_head).astype(jnp.bfloat16)
    back = jnp.concatenate(
        [grad_pooled, jnp.broadcast_to(scores.astype(jnp.bfloat16)[:, None], (dp_count * capacity, 128))],
        1,
    )
    back = lax.all_to_all(
        back.reshape(dp_count, capacity, width_view + 128), DP, split_axis=0, concat_axis=0, tiled=True
    ).reshape(dp_count * capacity, width_view + 128)
    back = dot_first(select, back)
    own_scores = back[:, width_view].astype(jnp.bfloat16)
    pixel_grad = crop_back(
        back[:, :width_view], crop_normed, crop_inverse, reward_norm_gain, patch_embed_weight, TILE
    )
    output_gradient = tail_backward(
        pixel_grad,
        decoded,
        normed,
        inverse_std,
        branch_gate,
        final_norm_scale,
        velocity_weight,
        decoder_weight,
    )
    rank_grad = product_final(output_gradient, adapter_up).astype(jnp.bfloat16)
    grad_b = dot_first(lowrank_adapter.astype(jnp.bfloat16), output_gradient)
    grad_b = jnp.concatenate([grad_b[:, :half], grad_b[:, half:]], 0)
    first = mp == 0
    grad_kept, grad_taken = dot_first(rank_grad, kept), dot_first(rank_grad, taken)
    grad_a = jnp.concatenate(
        [jnp.where(first, grad_kept, grad_taken), jnp.where(first, grad_taken, grad_kept)], 0
    )
    lead = group == 0
    mine = jnp.where(lead, grad_a, grad_b)
    given_part = jnp.where(lead, grad_b, grad_a).astype(jnp.bfloat16)
    mine = mine + swap_cores(given_part).astype(jnp.float32)
    pieces = jnp.pad(mine.astype(jnp.bfloat16), ((0, 0), (0, -half % 128))).reshape(128, -1, 128)
    parts = lax.all_to_all(pieces, CHIPS, split_axis=0, concat_axis=0, tiled=True)
    total = jnp.sum(parts.astype(jnp.float32), 0, keepdims=True).astype(jnp.bfloat16)
    total = lax.all_to_all(
        jnp.broadcast_to(total, parts.shape), CHIPS, split_axis=0, concat_axis=0, tiled=True
    )
    passed = swap_cores(total)
    total_a = jnp.where(lead, total, passed).reshape(128, -1)[:, :half]
    total_b = jnp.where(lead, passed, total).reshape(128, -1)[:, :half]
    rank = adapter_up.shape[0]
    grad_a = lax.dynamic_slice_in_dim(total_a, mp * rank, rank, 0).astype(jnp.float32).T
    grad_b = jnp.concatenate([total_b[:rank], total_b[rank:]], 1).astype(jnp.float32)
    return (grad_a, grad_b, own_scores)


def solution(mesh):
    fine = Mesh(mesh.devices.reshape(2, 4, 2, 8, 2), ("group", "x", "yl", "z", "mp"))
    dp = ("x", "yl", "z")
    rows = ("group",) + dp
    return jax.shard_map(
        shards,
        mesh=fine,
        in_specs=(
            P(rows, "mp"),
            P(rows + ("mp",), None),
            P("mp", dp),
            P("mp", None),
            P(),
            P(),
            P(),
            P(),
            P(),
            P(),
            P(rows + ("mp",), None),
            P(),
            P(),
            P(),
            P(),
            P(dp, None, None),
            P(rows + ("mp",), None),
            P(rows + ("mp",), None),
        ),
        out_specs=(P("mp", None), P(), P(rows + ("mp",))),
        check_vma=False,
    )
```

```python
import jax
import jax.numpy as jnp
from jax import lax
from jax.sharding import Mesh
from jax.sharding import PartitionSpec as P

TILE = 8


epsilon = 1e-06
sigma_last = 0.7
loss_weight = 16.0


def product_final(left, right):
    return lax.dot_general(
        left, right, (((1,), (1,)), ((), ())), preferred_element_type=jnp.float32
    )


def dot_first(left, right):
    return lax.dot_general(
        left, right, (((0,), (0,)), ((), ())), preferred_element_type=jnp.float32
    )


def normalize(values):
    centre = values - jnp.mean(values, -1, keepdims=True)
    inverse_std = lax.rsqrt(jnp.mean(centre * centre, -1, keepdims=True) + epsilon)
    return (centre * inverse_std, inverse_std)


def norm_back(grad_normed, normed, inverse_std):
    grad_mean = jnp.mean(grad_normed, -1, keepdims=True)
    cross_mean = jnp.mean(grad_normed * normed, -1, keepdims=True)
    return (grad_normed - grad_mean - normed * cross_mean) * inverse_std


def tail_forward(
    projected_rows,
    resid,
    branch_gate,
    final_norm_scale,
    final_norm_shift,
    velocity_weight,
    velocity_bias,
    noised_latent_tokens,
    decoder_weight,
    decoder_bias,
):
    stream = resid.astype(jnp.float32) + branch_gate.astype(jnp.float32) * projected_rows
    normed, inverse_std = normalize(stream)
    modulated = (
        normed * (1.0 + final_norm_scale.astype(jnp.float32)) + final_norm_shift.astype(jnp.float32)
    ).astype(jnp.bfloat16)
    velocity = jnp.dot(
        modulated, velocity_weight, preferred_element_type=jnp.float32
    ) + velocity_bias.astype(jnp.float32)
    latent = noised_latent_tokens.astype(jnp.float32) - sigma_last * velocity
    inner = jnp.dot(
        latent.astype(jnp.bfloat16), decoder_weight, preferred_element_type=jnp.float32
    ) + decoder_bias.astype(jnp.float32)
    return (jnp.tanh(inner), normed, inverse_std)


def tail_backward(
    pixel_grad,
    decoded,
    normed,
    inverse_std,
    branch_gate,
    final_norm_scale,
    velocity_weight,
    decoder_weight,
):
    grad_inner = (pixel_grad.astype(jnp.float32) * (1.0 - decoded * decoded)).astype(jnp.bfloat16)
    grad_latent = product_final(grad_inner, decoder_weight)
    grad_velocity = (-sigma_last * grad_latent).astype(jnp.bfloat16)
    grad_modulated = product_final(grad_velocity, velocity_weight)
    grad_stream = norm_back(
        grad_modulated * (1.0 + final_norm_scale.astype(jnp.float32)), normed, inverse_std
    )
    return (branch_gate.astype(jnp.float32) * grad_stream).astype(jnp.bfloat16)


def crop_embed(pixels, patch_embed_weight, reward_norm_gain):
    count, tile_len, width = pixels.shape
    embedded = jnp.dot(
        pixels.reshape(count * tile_len, width),
        patch_embed_weight,
        preferred_element_type=jnp.float32,
    )
    normed, inverse_std = normalize(embedded)
    scaled = (normed * reward_norm_gain.astype(jnp.float32)).reshape(
        count, tile_len, embedded.shape[1]
    )
    return (jnp.mean(scaled, 1).astype(jnp.bfloat16), normed, inverse_std)


def crop_score(query, text):
    text_wide = text.astype(jnp.float32)
    width = query.shape[-1]
    query_rms = jnp.sqrt(jnp.mean(query * query, -1, keepdims=True) + epsilon)
    text_rms = jnp.sqrt(jnp.mean(text_wide * text_wide, -1, keepdims=True) + epsilon)
    scores = jnp.mean(query * text_wide, -1, keepdims=True) / (query_rms * text_rms)
    grad_query = -loss_weight * (
        text_wide / (width * query_rms * text_rms)
        - scores * query / (width * query_rms * query_rms)
    )
    return (scores[:, 0], grad_query.astype(jnp.bfloat16))


def crop_back(grad_pooled, normed, inverse_std, reward_norm_gain, patch_embed_weight, tile_len):
    count, width = grad_pooled.shape
    spread = jnp.broadcast_to(
        (grad_pooled / tile_len)[:, None, :], (count, tile_len, width)
    ).reshape(count * tile_len, width)
    grad_embedded = norm_back(
        spread * reward_norm_gain.astype(jnp.float32), normed, inverse_std
    ).astype(jnp.bfloat16)
    return product_final(grad_embedded, patch_embed_weight).astype(jnp.bfloat16)


PLANE = ("x", "yl", "mp")
DP = ("x", "yl", "z")


def shift(block, axis, size, step):
    return lax.ppermute(block, axis, [(i, (i + step) % size) for i in range(size)])


def ring(block, axis, size):
    held = [(0, block)]
    up = down = block
    for step in range(1, size // 2):
        up, down = shift(up, axis, size, 1), shift(down, axis, size, -1)
        held += [(-step, up), (step, down)]
    half = block.shape[0] // 2
    if half == 0 or block.shape[0] % 2:
        held.append((size // 2, shift(up, axis, size, 1)))
    else:
        first = shift(up[:half], axis, size, 1)
        second = shift(down[half:], axis, size, -1)
        held.append((size // 2, jnp.concatenate([first, second], 0)))
    return held


def lay_rows(blocks, rows, size):
    filled = jnp.zeros((size, blocks[0].shape[1]), blocks[0].dtype)
    for first, block in zip(rows, blocks):
        filled = lax.dynamic_update_slice_in_dim(filled, block, first, 0)
    return filled


def place(blocks, axis, size):
    own = lax.axis_index(axis)
    shape = blocks[0][1].shape
    filled = jnp.zeros((size,) + shape, blocks[0][1].dtype)
    for offset, block in blocks:
        filled = lax.dynamic_update_index_in_dim(filled, block, (own + offset + size) % size, 0)
    return filled


def swap_cores(block):
    return lax.ppermute(block, "group", [(0, 1), (1, 0)])


def gather_weight(shard):
    picked = lax.ppermute(shard, ("group", "mp"), [(0, 0), (2, 1), (1, 2), (3, 3)])
    beside = shift(picked, "yl", 2, 1)
    pair = jnp.where(
        lax.axis_index("yl") == 0, jnp.stack([picked, beside]), jnp.stack([beside, picked])
    )
    columns, width = shard.shape
    along_z = place(ring(pair, "z", 8), "z", 8)
    block = jnp.transpose(along_z, (1, 0, 2, 3)).reshape(16 * columns, width)
    half = block.shape[0] // 2
    front, rear = block[:half], block[half:]
    up_front, down_rear = shift(front, "x", 4, 1), shift(rear, "x", 4, -1)
    up_rear, down_front = shift(rear, "x", 4, 1), shift(front, "x", 4, -1)
    far_front, far_rear = shift(up_front, "x", 4, 1), shift(down_rear, "x", 4, -1)
    own = lax.axis_index("x")
    held, rows = [block], [own * 2 * half]
    for offset, first, part in (
        (-1, 0, up_front),
        (1, half, down_rear),
        (-1, half, up_rear),
        (1, 0, down_front),
        (2, 0, far_front),
        (2, half, far_rear),
    ):
        held.append(part)
        rows.append(((own + offset + 4) % 4) * 2 * half + first)
    other = [swap_cores(part) for part in held]
    size = 64 * columns
    return lay_rows(held, rows, size), lay_rows(other, rows, size), pair, up_front


def exchange(pieces, axes):
    return lax.all_to_all(pieces, axes, split_axis=0, concat_axis=0, tiled=True)


def add_over_chips(part):
    width = part.shape[1]
    held = exchange(part.astype(jnp.bfloat16).reshape(16, 8, width), PLANE)
    share = jnp.sum(held.astype(jnp.float32), 0, keepdims=True).astype(jnp.bfloat16)
    held = exchange(jnp.broadcast_to(share, (8, 8, width)), "z")
    share = jnp.sum(held.astype(jnp.float32), 0, keepdims=True).astype(jnp.bfloat16)
    held = exchange(jnp.broadcast_to(share, (16, 8, width)), PLANE)
    return held.reshape(128, width)


def shards(
    attention_result,
    resid,
    attention_output_weight,
    adapter_down,
    adapter_up,
    branch_gate,
    final_norm_scale,
    final_norm_shift,
    velocity_weight,
    velocity_bias,
    noised_latent_tokens,
    decoder_weight,
    decoder_bias,
    patch_embed_weight,
    reward_norm_gain,
    reward_head_bank,
    prompt_features,
    assignment,
):
    group, mp = lax.axis_index("group"), lax.axis_index("mp")
    row_count, width = resid.shape
    half = width // 2
    tiles_dev = row_count // TILE
    weight_own, weight_other, pair, first_part = gather_weight(attention_output_weight.T)
    kept = lax.dynamic_slice_in_dim(attention_result, mp * row_count, row_count, 0)
    given = lax.dynamic_slice_in_dim(attention_result, (1 - mp) * row_count, row_count, 0)
    given, down_sent, _ = lax.optimization_barrier((given, adapter_down, pair))
    texts_sent, _ = lax.optimization_barrier((prompt_features, first_part))
    taken = shift(given, "mp", 2, 1)
    down_other = shift(down_sent, "mp", 2, 1)

    dp_count = 64
    capacity = 2
    target = assignment[:, 0]
    earlier = jnp.arange(tiles_dev)[None, :] < jnp.arange(tiles_dev)[:, None]
    matches = jnp.logical_and(target[:, None] == target[None, :], earlier)
    slot_index = jnp.sum(matches.astype(jnp.int32), 1)
    position = target * capacity + slot_index
    select = (
        jnp.arange(dp_count * capacity, dtype=jnp.int32)[:, None] == position[None, :]
    ).astype(jnp.bfloat16)
    texts = jnp.dot(select, texts_sent, preferred_element_type=jnp.float32)
    texts = texts.astype(jnp.bfloat16).reshape(dp_count, capacity, prompt_features.shape[1])
    crop_texts = lax.all_to_all(texts, DP, split_axis=0, concat_axis=0, tiled=True)

    same = group == mp
    for_own = jnp.where(same, kept, taken)
    for_other = jnp.where(same, taken, kept)
    lowrank_adapter = jnp.dot(kept, adapter_down, preferred_element_type=jnp.float32) + jnp.dot(
        taken, down_other, preferred_element_type=jnp.float32
    )
    projected_rows = (
        product_final(for_own, weight_own)
        + product_final(for_other, weight_other)
        + jnp.dot(
            lowrank_adapter, adapter_up.astype(jnp.float32), precision=lax.Precision.HIGHEST
        )
    )
    decoded, normed, inverse_std = tail_forward(
        projected_rows,
        resid,
        branch_gate,
        final_norm_scale,
        final_norm_shift,
        velocity_weight,
        velocity_bias,
        noised_latent_tokens,
        decoder_weight,
        decoder_bias,
    )
    pixels = decoded.astype(jnp.bfloat16)
    width_pix = pixels.shape[1]
    pooled, crop_normed, crop_inverse = crop_embed(
        pixels.reshape(tiles_dev, TILE, width_pix), patch_embed_weight, reward_norm_gain
    )
    width_view = pooled.shape[1]
    packed = jnp.dot(select, pooled, preferred_element_type=jnp.float32).astype(jnp.bfloat16)
    own_head = reward_head_bank[0]
    crop_pooled = lax.all_to_all(
        packed.reshape(dp_count, capacity, width_view), DP, split_axis=0, concat_axis=0, tiled=True
    ).reshape(dp_count * capacity, width_view)
    query = jnp.dot(crop_pooled, own_head, preferred_element_type=jnp.float32)
    scores, grad_query = crop_score(query, crop_texts.reshape(dp_count * capacity, -1))
    grad_pooled = product_final(grad_query, own_head).astype(jnp.bfloat16)
    back = jnp.concatenate(
        [grad_pooled, jnp.broadcast_to(scores.astype(jnp.bfloat16)[:, None], (dp_count * capacity, 128))],
        1,
    )
    back = lax.all_to_all(
        back.reshape(dp_count, capacity, width_view + 128), DP, split_axis=0, concat_axis=0, tiled=True
    ).reshape(dp_count * capacity, width_view + 128)
    back = dot_first(select, back)
    own_scores = back[:, width_view].astype(jnp.bfloat16)
    pixel_grad = crop_back(
        back[:, :width_view], crop_normed, crop_inverse, reward_norm_gain, patch_embed_weight, TILE
    )
    output_gradient = tail_backward(
        pixel_grad,
        decoded,
        normed,
        inverse_std,
        branch_gate,
        final_norm_scale,
        velocity_weight,
        decoder_weight,
    )
    rank_grad = product_final(output_gradient, adapter_up).astype(jnp.bfloat16)
    grad_b = dot_first(lowrank_adapter.astype(jnp.bfloat16), output_gradient)
    grad_b = jnp.concatenate([grad_b[:, :half], grad_b[:, half:]], 0)
    first = mp == 0
    grad_kept, grad_taken = dot_first(rank_grad, kept), dot_first(rank_grad, taken)
    grad_a = jnp.concatenate(
        [jnp.where(first, grad_kept, grad_taken), jnp.where(first, grad_taken, grad_kept)], 0
    )
    lead = group == 0
    mine = jnp.where(lead, grad_a, grad_b)
    given_part = jnp.where(lead, grad_b, grad_a).astype(jnp.bfloat16)
    mine = mine + swap_cores(given_part).astype(jnp.float32)
    total = add_over_chips(mine)
    passed = swap_cores(total)
    total_a = jnp.where(lead, total, passed)
    total_b = jnp.where(lead, passed, total)
    rank = adapter_up.shape[0]
    grad_a = lax.dynamic_slice_in_dim(total_a, mp * rank, rank, 0).astype(jnp.float32).T
    grad_b = jnp.concatenate([total_b[:rank], total_b[rank:]], 1).astype(jnp.float32)
    return (grad_a, grad_b, own_scores)


def solution(mesh):
    fine = Mesh(mesh.devices.reshape(2, 4, 2, 8, 2), ("group", "x", "yl", "z", "mp"))
    dp = ("x", "yl", "z")
    rows = ("group",) + dp
    return jax.shard_map(
        shards,
        mesh=fine,
        in_specs=(
            P(rows, "mp"),
            P(rows + ("mp",), None),
            P("mp", dp),
            P("mp", None),
            P(),
            P(),
            P(),
            P(),
            P(),
            P(),
            P(rows + ("mp",), None),
            P(),
            P(),
            P(),
            P(),
            P(dp, None, None),
            P(rows + ("mp",), None),
            P(rows + ("mp",), None),
        ),
        out_specs=(P("mp", None), P(), P(rows + ("mp",))),
        check_vma=False,
    )
```

```python
import jax
import jax.numpy as jnp
from jax import lax
from jax.experimental import pallas as pl
from jax.experimental.pallas import tpu as pltpu
from jax.sharding import Mesh
from jax.sharding import PartitionSpec as P

TILE = 8


epsilon = 1e-06
sigma_last = 0.7
loss_weight = 16.0


def product_final(left, right):
    return lax.dot_general(
        left, right, (((1,), (1,)), ((), ())), preferred_element_type=jnp.float32
    )


def normalize(values):
    centre = values - jnp.mean(values, -1, keepdims=True)
    inverse_std = lax.rsqrt(jnp.mean(centre * centre, -1, keepdims=True) + epsilon)
    return (centre * inverse_std, inverse_std)


def norm_back(grad_normed, normed, inverse_std):
    grad_mean = jnp.mean(grad_normed, -1, keepdims=True)
    cross_mean = jnp.mean(grad_normed * normed, -1, keepdims=True)
    return (grad_normed - grad_mean - normed * cross_mean) * inverse_std


def crop_score(query, text):
    text_wide = text.astype(jnp.float32)
    width = query.shape[-1]
    query_rms = jnp.sqrt(jnp.mean(query * query, -1, keepdims=True) + epsilon)
    text_rms = jnp.sqrt(jnp.mean(text_wide * text_wide, -1, keepdims=True) + epsilon)
    scores = jnp.mean(query * text_wide, -1, keepdims=True) / (query_rms * text_rms)
    grad_query = -loss_weight * (
        text_wide / (width * query_rms * text_rms)
        - scores * query / (width * query_rms * query_rms)
    )
    return (scores[:, 0], grad_query.astype(jnp.bfloat16))


PLANE = ("x", "yl", "mp")
DP = ("x", "yl", "z")


def shift(block, axis, size, step):
    return lax.ppermute(block, axis, [(i, (i + step) % size) for i in range(size)])


def ring(block, axis, size):
    held = [(0, block)]
    up = down = block
    for step in range(1, size // 2):
        up, down = shift(up, axis, size, 1), shift(down, axis, size, -1)
        held += [(-step, up), (step, down)]
    half = block.shape[0] // 2
    if half == 0 or block.shape[0] % 2:
        held.append((size // 2, shift(up, axis, size, 1)))
    else:
        first = shift(up[:half], axis, size, 1)
        second = shift(down[half:], axis, size, -1)
        held.append((size // 2, jnp.concatenate([first, second], 0)))
    return held


def place(blocks, axis, size):
    own = lax.axis_index(axis)
    shape = blocks[0][1].shape
    filled = jnp.zeros((size,) + shape, blocks[0][1].dtype)
    for offset, block in blocks:
        filled = lax.dynamic_update_index_in_dim(filled, block, (own + offset + size) % size, 0)
    return filled


def swap_cores(block):
    return lax.ppermute(block, "group", [(0, 1), (1, 0)])


def gather_weight(shard):
    picked = lax.ppermute(shard, ("group", "mp"), [(0, 0), (2, 1), (1, 2), (3, 3)])
    beside = shift(picked, "yl", 2, 1)
    pair = jnp.where(
        lax.axis_index("yl") == 0, jnp.stack([picked, beside]), jnp.stack([beside, picked])
    )
    columns, width = shard.shape
    along_z = place(ring(pair, "z", 8), "z", 8)
    half = 8 * columns
    front, rear = along_z[:, 0].reshape(half, width), along_z[:, 1].reshape(half, width)
    up_front, down_rear = shift(front, "x", 4, 1), shift(rear, "x", 4, -1)
    up_rear, down_front = shift(rear, "x", 4, 1), shift(front, "x", 4, -1)
    far_front, far_rear = shift(up_front, "x", 4, 1), shift(down_rear, "x", 4, -1)
    own = lax.axis_index("x")
    held, rows = [], []
    for offset, first, part in (
        (0, 0, front),
        (0, half, rear),
        (-1, 0, up_front),
        (1, half, down_rear),
        (-1, half, up_rear),
        (1, 0, down_front),
        (2, 0, far_front),
        (2, half, far_rear),
    ):
        held.append(part)
        rows.append(jnp.bitwise_and(own + offset + 4, 3) * 2 * half + first)
    other = [swap_cores(part) for part in held]
    return held + other, jnp.stack(rows).astype(jnp.int32), pair, up_rear


PARTS = 8
ROWS = 256


def product_sides(left, right):
    return lax.dot_general(
        left, right, (((0,), (1,)), ((), ())), preferred_element_type=jnp.float32
    )


def by_columns(array):
    return pl.BlockSpec((array.shape[0], ROWS), lambda i: (0, i))


def forward_kernel(
    place_ref,
    kept_ref,
    taken_ref,
    down_kept,
    down_taken,
    up_ref,
    resid_ref,
    gate_ref,
    gain_ref,
    bias_ref,
    velocity_ref,
    velocity_bias_ref,
    noised_ref,
    decoder_ref,
    decoder_bias_ref,
    embed_ref,
    norm_gain_ref,
    select_ref,
    *rest,
):
    parts = rest[: 2 * PARTS]
    lowrank_ref, normed_ref, inverse_ref, decoded_ref, crop_ref, crop_inverse_ref, packed_ref = rest[
        2 * PARTS : 2 * PARTS + 7
    ]
    weight, stream, pooled, sems = rest[2 * PARTS + 7 :]
    step = pl.program_id(0)
    height = parts[0].shape[0]
    copies = []
    for i, part in enumerate(parts):
        row = pl.multiple_of(place_ref[i % PARTS], 16)
        copies.append(
            pltpu.make_async_copy(part, weight.at[i // PARTS, pl.ds(row, height)], sems.at[i])
        )

    @pl.when(step == 0)
    def _():
        for copy in copies:
            copy.start()

    kept, taken = kept_ref[...], taken_ref[...]
    lowrank = product_sides(kept, down_kept[...]) + product_sides(taken, down_taken[...])
    high = lowrank.astype(jnp.bfloat16)
    low = (lowrank - high.astype(jnp.float32)).astype(jnp.bfloat16)
    lowrank_ref[...] = high

    @pl.when(step == 0)
    def _():
        for copy in copies:
            copy.wait()

    width = stream.shape[1]
    pairing = place_ref[PARTS]
    for first in range(0, width, 640):
        columns = slice(first, min(first + 640, width))
        projected = (
            product_sides(kept, weight[pairing, columns])
            + product_sides(taken, weight[1 - pairing, columns])
            + jnp.dot(high, up_ref[:, columns], preferred_element_type=jnp.float32)
            + jnp.dot(low, up_ref[:, columns], preferred_element_type=jnp.float32)
        )
        stream[:, columns] = (
            resid_ref[:, columns].astype(jnp.float32) + gate_ref[:, columns] * projected
        )
    count = 64
    for first in range(0, ROWS, count):
        rows = slice(first, first + count)
        normed, inverse_std = normalize(stream[rows, :])
        normed_ref[rows, :] = normed.astype(jnp.bfloat16)
        inverse_ref[rows, :] = inverse_std
        modulated = (normed * (1.0 + gain_ref[...]) + bias_ref[...]).astype(jnp.bfloat16)
        velocity = product_final(modulated, velocity_ref[...]) + velocity_bias_ref[...]
        latent = noised_ref[rows, :].astype(jnp.float32) - sigma_last * velocity
        inner = (
            jnp.dot(
                latent.astype(jnp.bfloat16), decoder_ref[...], preferred_element_type=jnp.float32
            )
            + decoder_bias_ref[...]
        )
        decoded_ref[rows, :] = jnp.tanh(inner)
    view = embed_ref.shape[1]
    embedded = jnp.dot(
        decoded_ref[...].astype(jnp.bfloat16), embed_ref[...], preferred_element_type=jnp.float32
    )
    crop_normed, crop_inverse = normalize(embedded)
    crop_ref[...] = crop_normed.astype(jnp.bfloat16)
    crop_inverse_ref[...] = crop_inverse
    scaled = (crop_normed * norm_gain_ref[...]).reshape(ROWS // TILE, TILE, view)
    crops = ROWS // TILE
    pooled[pl.ds(pl.multiple_of(step * crops, crops), crops), :] = jnp.mean(scaled, 1).astype(
        jnp.bfloat16
    )

    @pl.when(step == pl.num_programs(0) - 1)
    def _():
        packed_ref[...] = jnp.dot(
            select_ref[...], pooled[...], preferred_element_type=jnp.float32
        ).astype(jnp.bfloat16)


def whole(array):
    return pl.BlockSpec(array.shape, lambda i: (0,) * array.ndim)


def by_rows(array):
    return pl.BlockSpec((ROWS, array.shape[1]), lambda i: (i, 0))


def forward_call(place_rows, heads, downs, up, resid, gate, gain, bias, velocity_t, velocity_bias, noised, decoder, decoder_bias, embed, norm_gain, select, parts, interpret=False):
    count, width = resid.shape
    rank, view, pix = up.shape[0], embed.shape[1], embed.shape[0]
    shape = jax.ShapeDtypeStruct
    outs = (
        shape((count, rank), jnp.bfloat16),
        shape((count, width), jnp.bfloat16),
        shape((count, 1), jnp.float32),
        shape((count, pix), jnp.float32),
        shape((count, view), jnp.bfloat16),
        shape((count, 1), jnp.float32),
        shape((select.shape[0], view), jnp.bfloat16),
    )
    fixed = (gate, gain, bias, velocity_t, velocity_bias)
    return pl.pallas_call(
        forward_kernel,
        grid=(count // ROWS,),
        in_specs=[pl.BlockSpec(memory_space=pltpu.SMEM)]
        + [by_columns(heads[0])] * 2
        + [whole(downs[0])] * 2
        + [whole(up), by_rows(resid)]
        + [whole(a) for a in fixed]
        + [by_rows(noised)]
        + [whole(a) for a in (decoder, decoder_bias, embed, norm_gain, select)]
        + [pl.BlockSpec(memory_space=pl.ANY)] * len(parts),
        out_specs=[by_rows(a) for a in outs[:6]] + [whole(outs[6])],
        out_shape=outs,
        scratch_shapes=[
            pltpu.VMEM((2, width, heads[0].shape[0]), jnp.bfloat16),
            pltpu.VMEM((ROWS, width), jnp.float32),
            pltpu.VMEM((count // TILE, view), jnp.bfloat16),
            pltpu.SemaphoreType.DMA((2 * PARTS,)),
        ],
        compiler_params=pltpu.CompilerParams(vmem_limit_bytes=48 * 1024 * 1024),
        name="forward",
        interpret=interpret,
    )(place_rows, *heads, *downs, up, resid, *fixed, noised, decoder, decoder_bias, embed, norm_gain, select, *parts)


def backward_kernel(
    back_ref,
    pick_ref,
    crop_ref,
    crop_inverse_ref,
    norm_gain_ref,
    embed_ref,
    decoded_ref,
    decoder_ref,
    velocity_ref,
    gain_ref,
    gate_ref,
    normed_ref,
    inverse_ref,
    up_ref,
    lowrank_ref,
    kept_ref,
    taken_ref,
    grad_kept,
    grad_taken,
    grad_b,
    score_ref,
    output,
):
    step = pl.program_id(0)
    view = embed_ref.shape[1]
    crops = ROWS // TILE
    back = jnp.dot(pick_ref[...], back_ref[...], preferred_element_type=jnp.float32)
    score_ref[...] = back[:, view:]
    spread = jnp.broadcast_to((back[:, :view] / TILE)[:, None, :], (crops, TILE, view))
    spread = spread.reshape(ROWS, view) * norm_gain_ref[...]
    grad_embedded = norm_back(
        spread, crop_ref[...].astype(jnp.float32), crop_inverse_ref[...]
    ).astype(jnp.bfloat16)
    pixel_grad = product_final(grad_embedded, embed_ref[...]).astype(jnp.bfloat16)
    decoded = decoded_ref[...]
    grad_inner = (pixel_grad.astype(jnp.float32) * (1.0 - decoded * decoded)).astype(jnp.bfloat16)
    grad_velocity = (-sigma_last * product_final(grad_inner, decoder_ref[...])).astype(jnp.bfloat16)
    count = 64
    for first in range(0, ROWS, count):
        rows = slice(first, first + count)
        grad_modulated = jnp.dot(
            grad_velocity[rows, :], velocity_ref[...], preferred_element_type=jnp.float32
        )
        grad_stream = norm_back(
            grad_modulated * (1.0 + gain_ref[...]),
            normed_ref[rows, :].astype(jnp.float32),
            inverse_ref[rows, :],
        )
        output[rows, :] = (gate_ref[...] * grad_stream).astype(jnp.bfloat16)
    rank_grad = product_final(up_ref[...], output[...]).astype(jnp.bfloat16)
    kept = product_final(rank_grad, kept_ref[...])
    taken = product_final(rank_grad, taken_ref[...])
    up_part = jnp.dot(lowrank_ref[...], output[...], preferred_element_type=jnp.float32)

    @pl.when(step == 0)
    def _():
        grad_kept[...] = kept
        grad_taken[...] = taken
        grad_b[...] = up_part

    @pl.when(step > 0)
    def _():
        grad_kept[...] += kept
        grad_taken[...] += taken
        grad_b[...] += up_part


def backward_call(back, pick, crop_normed, crop_inverse, norm_gain, embed, decoded, decoder, velocity_t, gain, gate, normed, inverse, up, lowrank_t, heads, interpret=False):
    count, width = normed.shape
    rank, half = up.shape[0], heads[0].shape[0]
    shape = jax.ShapeDtypeStruct
    crops = ROWS // TILE
    outs = (
        shape((rank, half), jnp.float32),
        shape((rank, half), jnp.float32),
        shape((rank, width), jnp.float32),
        shape((count // TILE, 128), jnp.float32),
    )
    return pl.pallas_call(
        backward_kernel,
        grid=(count // ROWS,),
        in_specs=[
            whole(back),
            pl.BlockSpec((crops, pick.shape[1]), lambda i: (i, 0)),
            by_rows(crop_normed),
            by_rows(crop_inverse),
            whole(norm_gain),
            whole(embed),
            by_rows(decoded),
            whole(decoder),
            whole(velocity_t),
            whole(gain),
            whole(gate),
            by_rows(normed),
            by_rows(inverse),
            whole(up),
            pl.BlockSpec((rank, ROWS), lambda i: (0, i)),
            by_columns(heads[0]),
            by_columns(heads[1]),
        ],
        out_specs=[whole(a) for a in outs[:3]] + [pl.BlockSpec((crops, 128), lambda i: (i, 0))],
        out_shape=outs,
        scratch_shapes=[pltpu.VMEM((ROWS, width), jnp.bfloat16)],
        compiler_params=pltpu.CompilerParams(vmem_limit_bytes=48 * 1024 * 1024),
        name="backward",
        interpret=interpret,
    )(back, pick, crop_normed, crop_inverse, norm_gain, embed, decoded, decoder, velocity_t, gain, gate, normed, inverse, up, lowrank_t, *heads)


def exchange(pieces, axes):
    return lax.all_to_all(pieces, axes, split_axis=0, concat_axis=0, tiled=True)


def add_over_chips(part):
    width = part.shape[1]
    held = exchange(part.astype(jnp.bfloat16).reshape(16, 8, width), PLANE)
    share = jnp.sum(held.astype(jnp.float32), 0, keepdims=True).astype(jnp.bfloat16)
    held = exchange(jnp.broadcast_to(share, (8, 8, width)), "z")
    share = jnp.sum(held.astype(jnp.float32), 0, keepdims=True).astype(jnp.bfloat16)
    held = exchange(jnp.broadcast_to(share, (16, 8, width)), PLANE)
    return held.reshape(128, width)


def shards(
    attention_result,
    resid,
    attention_output_weight,
    adapter_down,
    adapter_up,
    branch_gate,
    final_norm_scale,
    final_norm_shift,
    velocity_weight,
    velocity_bias,
    noised_latent_tokens,
    decoder_weight,
    decoder_bias,
    patch_embed_weight,
    reward_norm_gain,
    reward_head_bank,
    prompt_features,
    assignment,
):
    group, mp = lax.axis_index("group"), lax.axis_index("mp")
    row_count, width = resid.shape
    half = width // 2
    tiles_dev = row_count // TILE
    parts, part_rows, early, late = gather_weight(attention_output_weight.T)
    heads_t = attention_result.T
    kept = lax.dynamic_slice_in_dim(heads_t, mp * row_count, row_count, 1)
    given = lax.dynamic_slice_in_dim(heads_t, (1 - mp) * row_count, row_count, 1)
    given, down_sent, _ = lax.optimization_barrier((given, adapter_down.T, early))
    texts_sent, _ = lax.optimization_barrier((prompt_features, late))
    taken = shift(given, "mp", 2, 1)
    down_taken = shift(down_sent, "mp", 2, 1)

    dp_count = 64
    capacity = 2
    target = assignment[:, 0]
    earlier = jnp.arange(tiles_dev)[None, :] < jnp.arange(tiles_dev)[:, None]
    matches = jnp.logical_and(target[:, None] == target[None, :], earlier)
    slot_index = jnp.sum(matches.astype(jnp.int32), 1)
    position = target * capacity + slot_index
    select = (
        jnp.arange(dp_count * capacity, dtype=jnp.int32)[:, None] == position[None, :]
    ).astype(jnp.bfloat16)
    texts = jnp.dot(select, texts_sent, preferred_element_type=jnp.float32)
    texts = texts.astype(jnp.bfloat16).reshape(dp_count, capacity, prompt_features.shape[1])
    crop_texts = lax.all_to_all(texts, DP, split_axis=0, concat_axis=0, tiled=True)

    same = group == mp
    heads = (kept, taken)
    downs = (adapter_down.T, down_taken)
    pairing = jnp.where(same, 0, 1).astype(jnp.int32)[None]

    def row(vector):
        return vector.astype(jnp.float32)[None, :]

    velocity_t = velocity_weight.T
    lowrank, normed, inverse_std, decoded, crop_normed, crop_inverse, packed = forward_call(
        jnp.concatenate([part_rows, pairing]),
        heads,
        downs,
        adapter_up,
        resid,
        row(branch_gate),
        row(final_norm_scale),
        row(final_norm_shift),
        velocity_t,
        row(velocity_bias),
        noised_latent_tokens,
        decoder_weight,
        row(decoder_bias),
        patch_embed_weight,
        row(reward_norm_gain),
        select,
        parts,
    )
    width_view = packed.shape[1]
    own_head = reward_head_bank[0]
    crop_pooled = lax.all_to_all(
        packed.reshape(dp_count, capacity, width_view), DP, split_axis=0, concat_axis=0, tiled=True
    ).reshape(dp_count * capacity, width_view)
    query = jnp.dot(crop_pooled, own_head, preferred_element_type=jnp.float32)
    scores, grad_query = crop_score(query, crop_texts.reshape(dp_count * capacity, -1))
    grad_pooled = product_final(grad_query, own_head).astype(jnp.bfloat16)
    back = jnp.concatenate(
        [grad_pooled, jnp.broadcast_to(scores.astype(jnp.bfloat16)[:, None], (dp_count * capacity, 128))],
        1,
    )
    back = lax.all_to_all(
        back.reshape(dp_count, capacity, width_view + 128), DP, split_axis=0, concat_axis=0, tiled=True
    ).reshape(dp_count * capacity, width_view + 128)
    grad_kept, grad_taken, grad_b, scores_wide = backward_call(
        back,
        select.T,
        crop_normed,
        crop_inverse,
        row(reward_norm_gain),
        patch_embed_weight,
        decoded,
        decoder_weight,
        velocity_t,
        row(final_norm_scale),
        row(branch_gate),
        normed,
        inverse_std,
        adapter_up,
        lowrank.T,
        heads,
    )
    own_scores = scores_wide[:, 0].astype(jnp.bfloat16)
    grad_b = jnp.concatenate([grad_b[:, :half], grad_b[:, half:]], 0)
    lead, front = group == 0, mp == 0
    grad_a = jnp.concatenate(
        [jnp.where(front, grad_kept, grad_taken), jnp.where(front, grad_taken, grad_kept)], 0
    )
    mine = jnp.where(lead, grad_a, grad_b)
    given_part = jnp.where(lead, grad_b, grad_a).astype(jnp.bfloat16)
    mine = mine + swap_cores(given_part).astype(jnp.float32)
    total = add_over_chips(mine)
    passed = swap_cores(total)
    total_a = jnp.where(lead, total, passed)
    total_b = jnp.where(lead, passed, total)
    rank = adapter_up.shape[0]
    grad_a = lax.dynamic_slice_in_dim(total_a, mp * rank, rank, 0).astype(jnp.float32).T
    grad_b = jnp.concatenate([total_b[:rank], total_b[rank:]], 1).astype(jnp.float32)
    return (grad_a, grad_b, own_scores)


def solution(mesh):
    fine = Mesh(mesh.devices.reshape(2, 4, 2, 8, 2), ("group", "x", "yl", "z", "mp"))
    dp = ("x", "yl", "z")
    rows = ("group",) + dp
    return jax.shard_map(
        shards,
        mesh=fine,
        in_specs=(
            P(rows, "mp"),
            P(rows + ("mp",), None),
            P("mp", dp),
            P("mp", None),
            P(),
            P(),
            P(),
            P(),
            P(),
            P(),
            P(rows + ("mp",), None),
            P(),
            P(),
            P(),
            P(),
            P(dp, None, None),
            P(rows + ("mp",), None),
            P(rows + ("mp",), None),
        ),
        out_specs=(P("mp", None), P(), P(rows + ("mp",))),
        check_vma=False,
    )
```

```python
import jax
import jax.numpy as jnp
from jax import lax
from jax.experimental import pallas as pl
from jax.experimental.pallas import tpu as pltpu
from jax.sharding import Mesh
from jax.sharding import PartitionSpec as P

TILE = 8


epsilon = 1e-06
sigma_last = 0.7
loss_weight = 16.0


def product(left, right):
    return jnp.dot(left, right, preferred_element_type=jnp.float32)


def product_final(left, right):
    return lax.dot_general(
        left, right, (((1,), (1,)), ((), ())), preferred_element_type=jnp.float32
    )


def normalize(values):
    centre = values - jnp.mean(values, -1, keepdims=True)
    inverse_std = lax.rsqrt(jnp.mean(centre * centre, -1, keepdims=True) + epsilon)
    return (centre * inverse_std, inverse_std)


def norm_back(grad_normed, normed, inverse_std):
    grad_mean = jnp.mean(grad_normed, -1, keepdims=True)
    cross_mean = jnp.mean(grad_normed * normed, -1, keepdims=True)
    return (grad_normed - grad_mean - normed * cross_mean) * inverse_std


def crop_score(query, text):
    text_wide = text.astype(jnp.float32)
    width = query.shape[-1]
    query_rms = jnp.sqrt(jnp.mean(query * query, -1, keepdims=True) + epsilon)
    text_rms = jnp.sqrt(jnp.mean(text_wide * text_wide, -1, keepdims=True) + epsilon)
    scores = jnp.mean(query * text_wide, -1, keepdims=True) / (query_rms * text_rms)
    grad_query = -loss_weight * (
        text_wide / (width * query_rms * text_rms)
        - scores * query / (width * query_rms * query_rms)
    )
    return (scores[:, 0], grad_query.astype(jnp.bfloat16))


PLANE = ("x", "yl", "mp")
DP = ("x", "yl", "z")


def shift(block, axis, size, step):
    return lax.ppermute(block, axis, [(i, (i + step) % size) for i in range(size)])


def ring(block, axis, size):
    held = [(0, block)]
    up = down = block
    for step in range(1, size // 2):
        up, down = shift(up, axis, size, 1), shift(down, axis, size, -1)
        held += [(-step, up), (step, down)]
    half = block.shape[0] // 2
    if half == 0 or block.shape[0] % 2:
        held.append((size // 2, shift(up, axis, size, 1)))
    else:
        first = shift(up[:half], axis, size, 1)
        second = shift(down[half:], axis, size, -1)
        held.append((size // 2, jnp.concatenate([first, second], 0)))
    return held


def place(blocks, axis, size):
    own = lax.axis_index(axis)
    shape = blocks[0][1].shape
    filled = jnp.zeros((size,) + shape, blocks[0][1].dtype)
    for offset, block in blocks:
        filled = lax.dynamic_update_index_in_dim(filled, block, (own + offset + size) % size, 0)
    return filled


def swap_cores(block):
    return lax.ppermute(block, "group", [(0, 1), (1, 0)])


def gather_weight(shard):
    picked = lax.ppermute(shard, ("group", "mp"), [(0, 0), (2, 1), (1, 2), (3, 3)])
    beside = shift(picked, "yl", 2, 1)
    pair = jnp.where(
        lax.axis_index("yl") == 0, jnp.stack([picked, beside]), jnp.stack([beside, picked])
    )
    columns, width = shard.shape
    along_z = place(ring(pair, "z", 8), "z", 8)
    half = 8 * columns
    front, rear = along_z[:, 0].reshape(half, width), along_z[:, 1].reshape(half, width)
    up_front, down_rear = shift(front, "x", 4, 1), shift(rear, "x", 4, -1)
    up_rear, down_front = shift(rear, "x", 4, 1), shift(front, "x", 4, -1)
    return pair, (front, rear, up_front, down_rear, up_rear, down_front)


def finish_weight(held, ready):
    front, rear, up_front, down_rear, up_rear, down_front = held
    far_front, far_rear = shift(up_front, "x", 4, 1), shift(down_rear, "x", 4, -1)
    far_front, *ready = lax.optimization_barrier((far_front, *ready))
    own, half = lax.axis_index("x"), front.shape[0]
    held, rows = [], []
    for offset, first, part in (
        (0, 0, front),
        (0, half, rear),
        (-1, 0, up_front),
        (1, half, down_rear),
        (-1, half, up_rear),
        (1, 0, down_front),
        (2, 0, far_front),
        (2, half, far_rear),
    ):
        held.append(part)
        rows.append(jnp.bitwise_and(own + offset + 4, 3) * 2 * half + first)
    other = [swap_cores(part) for part in held]
    return held + other, jnp.stack(rows).astype(jnp.int32), ready


def pad_row(vector, width):
    return jnp.pad(vector.astype(jnp.float32), (0, width - vector.shape[0]))


PARTS = 8
ROWS = 256
PARTS_SPACE = pltpu.HBM


def product_first(left, right):
    return lax.dot_general(
        left, right, (((0,), (0,)), ((), ())), preferred_element_type=jnp.float32
    )


def by_columns(array):
    return pl.BlockSpec((array.shape[0], ROWS), lambda i: (0, i))


def forward_kernel(
    place_ref,
    kept_ref,
    taken_ref,
    down_kept,
    down_taken,
    up_ref,
    resid_ref,
    rows_ref,
    velocity_ref,
    noised_ref,
    decoder_ref,
    embed_ref,
    select_ref,
    *rest,
):
    parts = rest[: 2 * PARTS]
    lowrank_ref, normed_ref, stats_ref, decoded_ref, crop_ref, packed_ref = rest[
        2 * PARTS : 2 * PARTS + 6
    ]
    weight, stream, modulated, pooled, sems = rest[2 * PARTS + 6 :]
    step = pl.program_id(0)
    height = parts[0].shape[0]
    copies = []
    for i, part in enumerate(parts):
        row = pl.multiple_of(place_ref[i % PARTS], 16)
        copies.append(
            pltpu.make_async_copy(part, weight.at[i // PARTS, pl.ds(row, height)], sems.at[i])
        )

    @pl.when(step == 0)
    def _():
        for copy in copies:
            copy.start()

    kept, taken = kept_ref[...], taken_ref[...]
    lowrank = product(down_kept[...], kept) + product(down_taken[...], taken)
    high = lowrank.astype(jnp.bfloat16)
    low = (lowrank - high.astype(jnp.float32)).astype(jnp.bfloat16)
    lowrank_ref[...] = high
    both = jnp.concatenate([high, low], 1)

    @pl.when(step == 0)
    def _():
        for copy in copies:
            copy.wait()

    width = stream.shape[1]
    view, pix, latent_width = embed_ref.shape[1], embed_ref.shape[0], velocity_ref.shape[0]
    pairing = place_ref[PARTS]
    for first in range(0, width, 640):
        columns = slice(first, min(first + 640, width))
        adapted = product_first(up_ref[:, columns], both)
        projected = (
            product(weight[pairing, columns], kept)
            + product(weight[1 - pairing, columns], taken)
            + (adapted[:, :ROWS] + adapted[:, ROWS:])
        ).T
        stream[:, columns] = (
            resid_ref[:, columns].astype(jnp.float32) + rows_ref[0:1, columns] * projected
        )
    count = 64
    for first in range(0, ROWS, count):
        rows = slice(first, first + count)
        normed, inverse_std = normalize(stream[rows, :])
        normed_ref[rows, :] = normed.astype(jnp.bfloat16)
        stats_ref[rows, 0:1] = inverse_std
        modulated[rows, :] = (normed * (1.0 + rows_ref[1:2, :]) + rows_ref[2:3, :]).astype(
            jnp.bfloat16
        )
    velocity = product_final(modulated[...], velocity_ref[...]) + rows_ref[3:4, :latent_width]
    latent = noised_ref[...].astype(jnp.float32).T - sigma_last * velocity
    inner = product(latent.astype(jnp.bfloat16), decoder_ref[...]) + rows_ref[4:5, :pix]
    decoded = jnp.tanh(inner)
    decoded_ref[...] = decoded
    embedded = product(decoded.astype(jnp.bfloat16), embed_ref[...])
    crop_normed, crop_inverse = normalize(embedded)
    crop_ref[...] = crop_normed.astype(jnp.bfloat16)
    stats_ref[:, 1:2] = crop_inverse
    crops = ROWS // TILE
    scaled = (crop_normed * rows_ref[5:6, :view]).reshape(crops, TILE, view)
    pooled[pl.ds(pl.multiple_of(step * crops, crops), crops), :] = jnp.mean(scaled, 1).astype(
        jnp.bfloat16
    )

    @pl.when(step == pl.num_programs(0) - 1)
    def _():
        packed_ref[...] = product(select_ref[...], pooled[...]).astype(jnp.bfloat16)


def whole(array):
    return pl.BlockSpec(array.shape, lambda i: (0,) * array.ndim)


def by_rows(array):
    return pl.BlockSpec((ROWS, array.shape[1]), lambda i: (i, 0))


def forward_call(place_rows, heads, downs, up, resid, vectors, velocity_t, noised_t, decoder, embed, select, parts, interpret=False):
    count, width = resid.shape
    rank, view, pix = up.shape[0], embed.shape[1], embed.shape[0]
    shape = jax.ShapeDtypeStruct
    outs = (
        shape((rank, count), jnp.bfloat16),
        shape((count, width), jnp.bfloat16),
        shape((count, 128), jnp.float32),
        shape((count, pix), jnp.float32),
        shape((count, view), jnp.bfloat16),
        shape((select.shape[0], view), jnp.bfloat16),
    )
    return pl.pallas_call(
        forward_kernel,
        grid=(count // ROWS,),
        in_specs=[pl.BlockSpec(memory_space=pltpu.SMEM)]
        + [by_columns(heads[0])] * 2
        + [whole(downs[0])] * 2
        + [whole(up), by_rows(resid), whole(vectors), whole(velocity_t), by_columns(noised_t)]
        + [whole(a) for a in (decoder, embed, select)]
        + [pl.BlockSpec(memory_space=PARTS_SPACE)] * len(parts),
        out_specs=[by_columns(outs[0])] + [by_rows(a) for a in outs[1:5]] + [whole(outs[5])],
        out_shape=outs,
        scratch_shapes=[
            pltpu.VMEM((2, width, heads[0].shape[0]), jnp.bfloat16),
            pltpu.VMEM((ROWS, width), jnp.float32),
            pltpu.VMEM((ROWS, width), jnp.bfloat16),
            pltpu.VMEM((count // TILE, view), jnp.bfloat16),
            pltpu.SemaphoreType.DMA((2 * PARTS,)),
        ],
        compiler_params=pltpu.CompilerParams(vmem_limit_bytes=58 * 1024 * 1024),
        name="forward",
        interpret=interpret,
    )(place_rows, *heads, *downs, up, resid, vectors, velocity_t, noised_t, decoder, embed, select, *parts)


def backward_kernel(
    back_ref,
    pick_ref,
    crop_ref,
    stats_ref,
    rows_ref,
    embed_ref,
    decoded_ref,
    decoder_ref,
    velocity_ref,
    normed_ref,
    up_ref,
    lowrank_ref,
    kept_ref,
    taken_ref,
    grad_kept,
    grad_taken,
    grad_b,
    score_ref,
    output,
):
    step = pl.program_id(0)
    view = embed_ref.shape[1]
    crops = ROWS // TILE
    back = jnp.dot(pick_ref[...], back_ref[...], preferred_element_type=jnp.float32)
    score_ref[...] = back[:, view:]
    spread = jnp.broadcast_to((back[:, :view] / TILE)[:, None, :], (crops, TILE, view))
    spread = spread.reshape(ROWS, view) * rows_ref[5:6, :view]
    grad_embedded = norm_back(
        spread, crop_ref[...].astype(jnp.float32), stats_ref[:, 1:2]
    ).astype(jnp.bfloat16)
    pixel_grad = product_final(grad_embedded, embed_ref[...]).astype(jnp.bfloat16)
    decoded = decoded_ref[...]
    grad_inner = (pixel_grad.astype(jnp.float32) * (1.0 - decoded * decoded)).astype(jnp.bfloat16)
    grad_velocity = (-sigma_last * product_final(grad_inner, decoder_ref[...])).astype(jnp.bfloat16)
    count = 64
    for first in range(0, ROWS, count):
        rows = slice(first, first + count)
        grad_modulated = jnp.dot(
            grad_velocity[rows, :], velocity_ref[...], preferred_element_type=jnp.float32
        )
        grad_stream = norm_back(
            grad_modulated * (1.0 + rows_ref[1:2, :]),
            normed_ref[rows, :].astype(jnp.float32),
            stats_ref[rows, 0:1],
        )
        output[rows, :] = (rows_ref[0:1, :] * grad_stream).astype(jnp.bfloat16)
    rank_grad = product_final(up_ref[...], output[...]).astype(jnp.bfloat16)
    kept = product_final(rank_grad, kept_ref[...])
    taken = product_final(rank_grad, taken_ref[...])
    up_part = jnp.dot(lowrank_ref[...], output[...], preferred_element_type=jnp.float32)

    @pl.when(step == 0)
    def _():
        grad_kept[...] = kept
        grad_taken[...] = taken
        grad_b[...] = up_part

    @pl.when(step > 0)
    def _():
        grad_kept[...] += kept
        grad_taken[...] += taken
        grad_b[...] += up_part


def backward_call(back, pick, crop_normed, stats, vectors, embed, decoded, decoder, velocity_t, normed, up, lowrank_t, heads, interpret=False):
    count, width = normed.shape
    rank, half = up.shape[0], heads[0].shape[0]
    shape = jax.ShapeDtypeStruct
    crops = ROWS // TILE
    outs = (
        shape((rank, half), jnp.float32),
        shape((rank, half), jnp.float32),
        shape((rank, width), jnp.float32),
        shape((count // TILE, 128), jnp.float32),
    )
    return pl.pallas_call(
        backward_kernel,
        grid=(count // ROWS,),
        in_specs=[
            whole(back),
            pl.BlockSpec((crops, pick.shape[1]), lambda i: (i, 0)),
            by_rows(crop_normed),
            by_rows(stats),
            whole(vectors),
            whole(embed),
            by_rows(decoded),
            whole(decoder),
            whole(velocity_t),
            by_rows(normed),
            whole(up),
            pl.BlockSpec((rank, ROWS), lambda i: (0, i)),
            by_columns(heads[0]),
            by_columns(heads[1]),
        ],
        out_specs=[whole(a) for a in outs[:3]] + [pl.BlockSpec((crops, 128), lambda i: (i, 0))],
        out_shape=outs,
        scratch_shapes=[pltpu.VMEM((ROWS, width), jnp.bfloat16)],
        compiler_params=pltpu.CompilerParams(vmem_limit_bytes=58 * 1024 * 1024),
        name="backward",
        interpret=interpret,
    )(back, pick, crop_normed, stats, vectors, embed, decoded, decoder, velocity_t, normed, up, lowrank_t, *heads)


def exchange(pieces, axes):
    return lax.all_to_all(pieces, axes, split_axis=0, concat_axis=0, tiled=True)


def add_over_chips(part):
    width = part.shape[1]
    held = exchange(part.astype(jnp.bfloat16).reshape(16, 8, width), PLANE)
    share = jnp.sum(held.astype(jnp.float32), 0, keepdims=True).astype(jnp.bfloat16)
    held = exchange(jnp.broadcast_to(share, (8, 8, width)), "z")
    share = jnp.sum(held.astype(jnp.float32), 0, keepdims=True).astype(jnp.bfloat16)
    held = exchange(jnp.broadcast_to(share, (16, 8, width)), PLANE)
    return held.reshape(128, width)


def shards(
    attention_result,
    resid,
    attention_output_weight,
    adapter_down,
    adapter_up,
    branch_gate,
    final_norm_scale,
    final_norm_shift,
    velocity_weight,
    velocity_bias,
    noised_latent_tokens,
    decoder_weight,
    decoder_bias,
    patch_embed_weight,
    reward_norm_gain,
    reward_head_bank,
    prompt_features,
    assignment,
):
    group, mp = lax.axis_index("group"), lax.axis_index("mp")
    row_count, width = resid.shape
    half = width // 2
    tiles_dev = row_count // TILE
    pair, held = gather_weight(attention_output_weight.T)
    heads_t = attention_result.T
    kept = lax.dynamic_slice_in_dim(heads_t, mp * row_count, row_count, 1)
    given = lax.dynamic_slice_in_dim(heads_t, (1 - mp) * row_count, row_count, 1)
    given, down_sent, _ = lax.optimization_barrier((given, adapter_down.T, pair))
    taken = shift(given, "mp", 2, 1)
    down_taken = shift(down_sent, "mp", 2, 1)

    _, small, prompts, names = lax.optimization_barrier(
        (
            held[2],
            (
                branch_gate,
                final_norm_scale,
                final_norm_shift,
                velocity_bias,
                decoder_bias,
                reward_norm_gain,
            ),
            prompt_features,
            assignment,
        )
    )

    dp_count = 64
    capacity = 2
    target = names[:, 0]
    earlier = jnp.arange(tiles_dev)[None, :] < jnp.arange(tiles_dev)[:, None]
    matches = jnp.logical_and(target[:, None] == target[None, :], earlier)
    slot_index = jnp.sum(matches.astype(jnp.int32), 1)
    position = target * capacity + slot_index
    select = (
        jnp.arange(dp_count * capacity, dtype=jnp.int32)[:, None] == position[None, :]
    ).astype(jnp.bfloat16)
    texts = jnp.dot(select, prompts, preferred_element_type=jnp.float32)
    texts = texts.astype(jnp.bfloat16).reshape(dp_count, capacity, prompt_features.shape[1])
    vectors = jnp.stack([pad_row(vector, width) for vector in small])
    pick = select.T
    crop_texts = lax.all_to_all(texts, DP, split_axis=0, concat_axis=0, tiled=True)
    parts, part_rows, (crop_texts, vectors, select, pick) = finish_weight(
        held, (crop_texts, vectors, select, pick)
    )

    same = group == mp
    heads = (kept, taken)
    downs = (adapter_down.T, down_taken)
    pairing = jnp.where(same, 0, 1).astype(jnp.int32)[None]

    velocity_t = velocity_weight.T
    lowrank_t, normed, stats, decoded, crop_normed, packed = forward_call(
        jnp.concatenate([part_rows, pairing]),
        heads,
        downs,
        adapter_up,
        resid,
        vectors,
        velocity_t,
        noised_latent_tokens.T,
        decoder_weight,
        patch_embed_weight,
        select,
        parts,
    )
    width_view = packed.shape[1]
    own_head = reward_head_bank[0]
    crop_pooled = lax.all_to_all(
        packed.reshape(dp_count, capacity, width_view), DP, split_axis=0, concat_axis=0, tiled=True
    ).reshape(dp_count * capacity, width_view)
    query = jnp.dot(crop_pooled, own_head, preferred_element_type=jnp.float32)
    scores, grad_query = crop_score(query, crop_texts.reshape(dp_count * capacity, -1))
    grad_pooled = product_final(grad_query, own_head).astype(jnp.bfloat16)
    back = jnp.concatenate(
        [grad_pooled, jnp.broadcast_to(scores.astype(jnp.bfloat16)[:, None], (dp_count * capacity, 128))],
        1,
    )
    back = lax.all_to_all(
        back.reshape(dp_count, capacity, width_view + 128), DP, split_axis=0, concat_axis=0, tiled=True
    ).reshape(dp_count * capacity, width_view + 128)
    grad_kept, grad_taken, grad_b, scores_wide = backward_call(
        back,
        pick,
        crop_normed,
        stats,
        vectors,
        patch_embed_weight,
        decoded,
        decoder_weight,
        velocity_t,
        normed,
        adapter_up,
        lowrank_t,
        heads,
    )
    own_scores = scores_wide[:, 0].astype(jnp.bfloat16)
    grad_b = jnp.concatenate([grad_b[:, :half], grad_b[:, half:]], 0)
    lead, front = group == 0, mp == 0
    grad_a = jnp.concatenate(
        [jnp.where(front, grad_kept, grad_taken), jnp.where(front, grad_taken, grad_kept)], 0
    )
    mine = jnp.where(lead, grad_a, grad_b)
    given_part = jnp.where(lead, grad_b, grad_a).astype(jnp.bfloat16)
    mine = mine + swap_cores(given_part).astype(jnp.float32)
    total = add_over_chips(mine)
    passed = swap_cores(total)
    total_a = jnp.where(lead, total, passed)
    total_b = jnp.where(lead, passed, total)
    rank = adapter_up.shape[0]
    grad_a = lax.dynamic_slice_in_dim(total_a, mp * rank, rank, 0).astype(jnp.float32).T
    grad_b = jnp.concatenate([total_b[:rank], total_b[rank:]], 1).astype(jnp.float32)
    return (grad_a, grad_b, own_scores)


def solution(mesh):
    fine = Mesh(mesh.devices.reshape(2, 4, 2, 8, 2), ("group", "x", "yl", "z", "mp"))
    dp = ("x", "yl", "z")
    rows = ("group",) + dp
    return jax.shard_map(
        shards,
        mesh=fine,
        in_specs=(
            P(rows, "mp"),
            P(rows + ("mp",), None),
            P("mp", dp),
            P("mp", None),
            P(),
            P(),
            P(),
            P(),
            P(),
            P(),
            P(rows + ("mp",), None),
            P(),
            P(),
            P(),
            P(),
            P(dp, None, None),
            P(rows + ("mp",), None),
            P(rows + ("mp",), None),
        ),
        out_specs=(P("mp", None), P(), P(rows + ("mp",))),
        check_vma=False,
    )
```

```python
import jax
import jax.numpy as jnp
from jax import lax
from jax.experimental import pallas as pl
from jax.experimental.pallas import tpu as pltpu
from jax.sharding import Mesh
from jax.sharding import PartitionSpec as P

TILE = 8


epsilon = 1e-06
sigma_last = 0.7
loss_weight = 16.0


def product(left, right):
    return jnp.dot(left, right, preferred_element_type=jnp.float32)


def product_final(left, right):
    return lax.dot_general(
        left, right, (((1,), (1,)), ((), ())), preferred_element_type=jnp.float32
    )


def normalize(values):
    centre = values - jnp.mean(values, -1, keepdims=True)
    inverse_std = lax.rsqrt(jnp.mean(centre * centre, -1, keepdims=True) + epsilon)
    return (centre * inverse_std, inverse_std)


def norm_back(grad_normed, normed, inverse_std):
    grad_mean = jnp.mean(grad_normed, -1, keepdims=True)
    cross_mean = jnp.mean(grad_normed * normed, -1, keepdims=True)
    return (grad_normed - grad_mean - normed * cross_mean) * inverse_std


def crop_score(query, text):
    text_wide = text.astype(jnp.float32)
    width = query.shape[-1]
    query_rms = jnp.sqrt(jnp.mean(query * query, -1, keepdims=True) + epsilon)
    text_rms = jnp.sqrt(jnp.mean(text_wide * text_wide, -1, keepdims=True) + epsilon)
    scores = jnp.mean(query * text_wide, -1, keepdims=True) / (query_rms * text_rms)
    grad_query = -loss_weight * (
        text_wide / (width * query_rms * text_rms)
        - scores * query / (width * query_rms * query_rms)
    )
    return (scores[:, 0], grad_query.astype(jnp.bfloat16))


PLANE = ("x", "yl", "mp")
DP = ("x", "yl", "z")


def shift(block, axis, size, step):
    return lax.ppermute(block, axis, [(i, (i + step) % size) for i in range(size)])


def ring(block, axis, size):
    held = [(0, block)]
    up = down = block
    for step in range(1, size // 2):
        up, down = shift(up, axis, size, 1), shift(down, axis, size, -1)
        held += [(-step, up), (step, down)]
    half = block.shape[0] // 2
    if half == 0 or block.shape[0] % 2:
        held.append((size // 2, shift(up, axis, size, 1)))
    else:
        first = shift(up[:half], axis, size, 1)
        second = shift(down[half:], axis, size, -1)
        held.append((size // 2, jnp.concatenate([first, second], 0)))
    return held


def place(blocks, axis, size):
    own = lax.axis_index(axis)
    shape = blocks[0][1].shape
    filled = jnp.zeros((size,) + shape, blocks[0][1].dtype)
    for offset, block in blocks:
        filled = lax.dynamic_update_index_in_dim(filled, block, (own + offset + size) % size, 0)
    return filled


def swap_cores(block):
    return lax.ppermute(block, "group", [(0, 1), (1, 0)])


def gather_weight(shard, given, down):
    picked = lax.ppermute(shard, ("group", "mp"), [(0, 0), (2, 1), (1, 2), (3, 3)])
    beside = shift(picked, "yl", 2, 1)
    pair = jnp.where(
        lax.axis_index("yl") == 0, jnp.stack([picked, beside]), jnp.stack([beside, picked])
    )
    columns, width = shard.shape
    down_taken = shift(down, "mp", 2, 1)
    given, down_taken, _ = lax.optimization_barrier((given, down_taken, pair))
    taken = shift(given, "mp", 2, 1)
    along_z = place(ring(pair, "z", 8), "z", 8)
    half = 8 * columns
    front, rear = along_z[:, 0].reshape(half, width), along_z[:, 1].reshape(half, width)
    up_front, down_rear = shift(front, "x", 4, 1), shift(rear, "x", 4, -1)
    front_later, rear_later, taken = lax.optimization_barrier((front, rear, taken))
    up_rear, down_front = shift(rear_later, "x", 4, 1), shift(front_later, "x", 4, -1)
    return taken, down_taken, (front, rear, up_front, down_rear, up_rear, down_front)


def finish_weight(held, ready):
    front, rear, up_front, down_rear, up_rear, down_front = held
    far_front, far_rear = shift(up_front, "x", 4, 1), shift(down_rear, "x", 4, -1)
    own, half = lax.axis_index("x"), front.shape[0]
    held, rows = [], []
    for offset, first, part in (
        (0, 0, front),
        (0, half, rear),
        (-1, 0, up_front),
        (1, half, down_rear),
        (-1, half, up_rear),
        (1, 0, down_front),
        (2, 0, far_front),
        (2, half, far_rear),
    ):
        held.append(part)
        rows.append(jnp.bitwise_and(own + offset + 4, 3) * 2 * half + first)
    *waited, ready = lax.optimization_barrier((*held[:5], ready))
    other = [swap_cores(part) for part in waited + held[5:]]
    return held + other, jnp.stack(rows).astype(jnp.int32), ready


def pad_row(vector, width):
    return jnp.pad(vector.astype(jnp.float32), (0, width - vector.shape[0]))


PARTS = 8
ROWS = 512
PARTS_SPACE = pltpu.HBM


def product_first(left, right):
    return lax.dot_general(
        left, right, (((0,), (0,)), ((), ())), preferred_element_type=jnp.float32
    )


def by_columns(array):
    return pl.BlockSpec((array.shape[0], ROWS), lambda i: (0, i))


def forward_kernel(
    place_ref,
    kept_ref,
    taken_ref,
    down_kept,
    down_taken,
    up_ref,
    resid_ref,
    rows_ref,
    velocity_ref,
    noised_ref,
    decoder_ref,
    embed_ref,
    select_ref,
    *rest,
):
    parts = rest[: 2 * PARTS]
    lowrank_ref, normed_ref, stats_ref, decoded_ref, crop_ref, packed_ref = rest[
        2 * PARTS : 2 * PARTS + 6
    ]
    weight, stream, modulated, pooled, sems = rest[2 * PARTS + 6 :]
    step = pl.program_id(0)
    height = parts[0].shape[0]
    copies = []
    for i, part in enumerate(parts):
        row = pl.multiple_of(place_ref[i % PARTS], 16)
        copies.append(
            pltpu.make_async_copy(part, weight.at[i // PARTS, pl.ds(row, height)], sems.at[i])
        )

    @pl.when(step == 0)
    def _():
        for copy in copies:
            copy.start()

    kept, taken = kept_ref[...], taken_ref[...]
    lowrank = product(down_kept[...], kept) + product(down_taken[...], taken)
    high = lowrank.astype(jnp.bfloat16)
    low = (lowrank - high.astype(jnp.float32)).astype(jnp.bfloat16)
    lowrank_ref[...] = high
    both = jnp.concatenate([high, low], 1)

    @pl.when(step == 0)
    def _():
        for copy in copies:
            copy.wait()

    width = stream.shape[1]
    view, pix, latent_width = embed_ref.shape[1], embed_ref.shape[0], velocity_ref.shape[0]
    pairing = place_ref[PARTS]
    for first in range(0, width, 640):
        columns = slice(first, min(first + 640, width))
        adapted = product_first(up_ref[:, columns], both)
        projected = (
            product(weight[pairing, columns], kept)
            + product(weight[1 - pairing, columns], taken)
            + (adapted[:, :ROWS] + adapted[:, ROWS:])
        ).T
        stream[:, columns] = (
            resid_ref[:, columns].astype(jnp.float32) + rows_ref[0:1, columns] * projected
        )
    count = 64
    for first in range(0, ROWS, count):
        rows = slice(first, first + count)
        normed, inverse_std = normalize(stream[rows, :])
        normed_ref[rows, :] = normed.astype(jnp.bfloat16)
        stats_ref[rows, 0:1] = inverse_std
        modulated[rows, :] = (normed * (1.0 + rows_ref[1:2, :]) + rows_ref[2:3, :]).astype(
            jnp.bfloat16
        )
    velocity = product_final(modulated[...], velocity_ref[...]) + rows_ref[3:4, :latent_width]
    latent = noised_ref[...].astype(jnp.float32).T - sigma_last * velocity
    inner = product(latent.astype(jnp.bfloat16), decoder_ref[...]) + rows_ref[4:5, :pix]
    decoded = jnp.tanh(inner)
    decoded_ref[...] = decoded
    embedded = product(decoded.astype(jnp.bfloat16), embed_ref[...])
    crop_normed, crop_inverse = normalize(embedded)
    crop_ref[...] = crop_normed.astype(jnp.bfloat16)
    stats_ref[:, 1:2] = crop_inverse
    crops = ROWS // TILE
    scaled = (crop_normed * rows_ref[5:6, :view]).reshape(crops, TILE, view)
    pooled[pl.ds(pl.multiple_of(step * crops, crops), crops), :] = jnp.mean(scaled, 1).astype(
        jnp.bfloat16
    )

    @pl.when(step == pl.num_programs(0) - 1)
    def _():
        packed_ref[...] = product(select_ref[...], pooled[...]).astype(jnp.bfloat16)


def whole(array):
    return pl.BlockSpec(array.shape, lambda i: (0,) * array.ndim)


def by_rows(array):
    return pl.BlockSpec((ROWS, array.shape[1]), lambda i: (i, 0))


def forward_call(place_rows, heads, downs, up, resid, vectors, velocity_t, noised_t, decoder, embed, select, parts, interpret=False):
    count, width = resid.shape
    rank, view, pix = up.shape[0], embed.shape[1], embed.shape[0]
    shape = jax.ShapeDtypeStruct
    outs = (
        shape((rank, count), jnp.bfloat16),
        shape((count, width), jnp.bfloat16),
        shape((count, 128), jnp.float32),
        shape((count, pix), jnp.float32),
        shape((count, view), jnp.bfloat16),
        shape((select.shape[0], view), jnp.bfloat16),
    )
    return pl.pallas_call(
        forward_kernel,
        grid=(count // ROWS,),
        in_specs=[pl.BlockSpec(memory_space=pltpu.SMEM)]
        + [by_columns(heads[0])] * 2
        + [whole(downs[0])] * 2
        + [whole(up), by_rows(resid), whole(vectors), whole(velocity_t), by_columns(noised_t)]
        + [whole(a) for a in (decoder, embed, select)]
        + [pl.BlockSpec(memory_space=PARTS_SPACE)] * len(parts),
        out_specs=[by_columns(outs[0])] + [by_rows(a) for a in outs[1:5]] + [whole(outs[5])],
        out_shape=outs,
        scratch_shapes=[
            pltpu.VMEM((2, width, heads[0].shape[0]), jnp.bfloat16),
            pltpu.VMEM((ROWS, width), jnp.float32),
            pltpu.VMEM((ROWS, width), jnp.bfloat16),
            pltpu.VMEM((count // TILE, view), jnp.bfloat16),
            pltpu.SemaphoreType.DMA((2 * PARTS,)),
        ],
        compiler_params=pltpu.CompilerParams(vmem_limit_bytes=58 * 1024 * 1024),
        name="forward",
        interpret=interpret,
    )(place_rows, *heads, *downs, up, resid, vectors, velocity_t, noised_t, decoder, embed, select, *parts)


def backward_kernel(
    back_ref,
    pick_ref,
    crop_ref,
    stats_ref,
    rows_ref,
    embed_ref,
    decoded_ref,
    decoder_ref,
    velocity_ref,
    normed_ref,
    up_ref,
    lowrank_ref,
    kept_ref,
    taken_ref,
    grad_kept,
    grad_taken,
    grad_b,
    score_ref,
    output,
):
    step = pl.program_id(0)
    view = embed_ref.shape[1]
    crops = ROWS // TILE
    back = jnp.dot(pick_ref[...], back_ref[...], preferred_element_type=jnp.float32)
    score_ref[...] = back[:, view:]
    spread = jnp.broadcast_to((back[:, :view] / TILE)[:, None, :], (crops, TILE, view))
    spread = spread.reshape(ROWS, view) * rows_ref[5:6, :view]
    grad_embedded = norm_back(
        spread, crop_ref[...].astype(jnp.float32), stats_ref[:, 1:2]
    ).astype(jnp.bfloat16)
    pixel_grad = product_final(grad_embedded, embed_ref[...]).astype(jnp.bfloat16)
    decoded = decoded_ref[...]
    grad_inner = (pixel_grad.astype(jnp.float32) * (1.0 - decoded * decoded)).astype(jnp.bfloat16)
    grad_velocity = (-sigma_last * product_final(grad_inner, decoder_ref[...])).astype(jnp.bfloat16)
    count = 64
    for first in range(0, ROWS, count):
        rows = slice(first, first + count)
        grad_modulated = jnp.dot(
            grad_velocity[rows, :], velocity_ref[...], preferred_element_type=jnp.float32
        )
        grad_stream = norm_back(
            grad_modulated * (1.0 + rows_ref[1:2, :]),
            normed_ref[rows, :].astype(jnp.float32),
            stats_ref[rows, 0:1],
        )
        output[rows, :] = (rows_ref[0:1, :] * grad_stream).astype(jnp.bfloat16)
    rank_grad = product_final(up_ref[...], output[...]).astype(jnp.bfloat16)
    kept = product_final(rank_grad, kept_ref[...])
    taken = product_final(rank_grad, taken_ref[...])
    up_part = jnp.dot(lowrank_ref[...], output[...], preferred_element_type=jnp.float32)

    @pl.when(step == 0)
    def _():
        grad_kept[...] = kept
        grad_taken[...] = taken
        grad_b[...] = up_part

    @pl.when(step > 0)
    def _():
        grad_kept[...] += kept
        grad_taken[...] += taken
        grad_b[...] += up_part


def backward_call(back, pick, crop_normed, stats, vectors, embed, decoded, decoder, velocity_t, normed, up, lowrank_t, heads, interpret=False):
    count, width = normed.shape
    rank, half = up.shape[0], heads[0].shape[0]
    shape = jax.ShapeDtypeStruct
    crops = ROWS // TILE
    outs = (
        shape((rank, half), jnp.float32),
        shape((rank, half), jnp.float32),
        shape((rank, width), jnp.float32),
        shape((count // TILE, 128), jnp.float32),
    )
    return pl.pallas_call(
        backward_kernel,
        grid=(count // ROWS,),
        in_specs=[
            whole(back),
            pl.BlockSpec((crops, pick.shape[1]), lambda i: (i, 0)),
            by_rows(crop_normed),
            by_rows(stats),
            whole(vectors),
            whole(embed),
            by_rows(decoded),
            whole(decoder),
            whole(velocity_t),
            by_rows(normed),
            whole(up),
            pl.BlockSpec((rank, ROWS), lambda i: (0, i)),
            by_columns(heads[0]),
            by_columns(heads[1]),
        ],
        out_specs=[whole(a) for a in outs[:3]] + [pl.BlockSpec((crops, 128), lambda i: (i, 0))],
        out_shape=outs,
        scratch_shapes=[pltpu.VMEM((ROWS, width), jnp.bfloat16)],
        compiler_params=pltpu.CompilerParams(vmem_limit_bytes=58 * 1024 * 1024),
        name="backward",
        interpret=interpret,
    )(back, pick, crop_normed, stats, vectors, embed, decoded, decoder, velocity_t, normed, up, lowrank_t, *heads)


def exchange(pieces, axes):
    return lax.all_to_all(pieces, axes, split_axis=0, concat_axis=0, tiled=True)


def add_over_chips(part):
    width = part.shape[1]
    held = exchange(part.astype(jnp.bfloat16).reshape(16, 8, width), PLANE)
    share = jnp.sum(held.astype(jnp.float32), 0, keepdims=True).astype(jnp.bfloat16)
    held = exchange(jnp.broadcast_to(share, (8, 8, width)), "z")
    share = jnp.sum(held.astype(jnp.float32), 0, keepdims=True).astype(jnp.bfloat16)
    held = exchange(jnp.broadcast_to(share, (16, 8, width)), PLANE)
    return held.reshape(128, width)


def shards(
    attention_result,
    resid,
    attention_output_weight,
    adapter_down,
    adapter_up,
    branch_gate,
    final_norm_scale,
    final_norm_shift,
    velocity_weight,
    velocity_bias,
    noised_latent_tokens,
    decoder_weight,
    decoder_bias,
    patch_embed_weight,
    reward_norm_gain,
    reward_head_bank,
    prompt_features,
    assignment,
):
    group, mp = lax.axis_index("group"), lax.axis_index("mp")
    row_count, width = resid.shape
    half = width // 2
    tiles_dev = row_count // TILE
    heads_t = attention_result.T
    kept = lax.dynamic_slice_in_dim(heads_t, mp * row_count, row_count, 1)
    given = lax.dynamic_slice_in_dim(heads_t, (1 - mp) * row_count, row_count, 1)
    taken, down_taken, held = gather_weight(attention_output_weight.T, given, adapter_down.T)

    _, small, prompts, names = lax.optimization_barrier(
        (
            held[2],
            (
                branch_gate,
                final_norm_scale,
                final_norm_shift,
                velocity_bias,
                decoder_bias,
                reward_norm_gain,
            ),
            prompt_features,
            assignment,
        )
    )

    dp_count = 64
    capacity = 2
    target = names[:, 0]
    earlier = jnp.arange(tiles_dev)[None, :] < jnp.arange(tiles_dev)[:, None]
    matches = jnp.logical_and(target[:, None] == target[None, :], earlier)
    slot_index = jnp.sum(matches.astype(jnp.int32), 1)
    position = target * capacity + slot_index
    select = (
        jnp.arange(dp_count * capacity, dtype=jnp.int32)[:, None] == position[None, :]
    ).astype(jnp.bfloat16)
    texts = jnp.dot(select, prompts, preferred_element_type=jnp.float32)
    texts = texts.astype(jnp.bfloat16).reshape(dp_count, capacity, prompt_features.shape[1])
    vectors = jnp.stack([pad_row(vector, width) for vector in small])
    pick = select.T
    crop_texts = lax.all_to_all(texts, DP, split_axis=0, concat_axis=0, tiled=True)
    parts, part_rows, (crop_texts, vectors, select, pick) = finish_weight(
        held, (crop_texts, vectors, select, pick)
    )

    same = group == mp
    heads = (kept, taken)
    downs = (adapter_down.T, down_taken)
    pairing = jnp.where(same, 0, 1).astype(jnp.int32)[None]

    velocity_t = velocity_weight.T
    lowrank_t, normed, stats, decoded, crop_normed, packed = forward_call(
        jnp.concatenate([part_rows, pairing]),
        heads,
        downs,
        adapter_up,
        resid,
        vectors,
        velocity_t,
        noised_latent_tokens.T,
        decoder_weight,
        patch_embed_weight,
        select,
        parts,
    )
    width_view = packed.shape[1]
    own_head = reward_head_bank[0]
    crop_pooled = lax.all_to_all(
        packed.reshape(dp_count, capacity, width_view), DP, split_axis=0, concat_axis=0, tiled=True
    ).reshape(dp_count * capacity, width_view)
    query = jnp.dot(crop_pooled, own_head, preferred_element_type=jnp.float32)
    scores, grad_query = crop_score(query, crop_texts.reshape(dp_count * capacity, -1))
    grad_pooled = product_final(grad_query, own_head).astype(jnp.bfloat16)
    back = jnp.concatenate(
        [grad_pooled, jnp.broadcast_to(scores.astype(jnp.bfloat16)[:, None], (dp_count * capacity, 128))],
        1,
    )
    back = lax.all_to_all(
        back.reshape(dp_count, capacity, width_view + 128), DP, split_axis=0, concat_axis=0, tiled=True
    ).reshape(dp_count * capacity, width_view + 128)
    grad_kept, grad_taken, grad_b, scores_wide = backward_call(
        back,
        pick,
        crop_normed,
        stats,
        vectors,
        patch_embed_weight,
        decoded,
        decoder_weight,
        velocity_t,
        normed,
        adapter_up,
        lowrank_t,
        heads,
    )
    own_scores = scores_wide[:, 0].astype(jnp.bfloat16)
    grad_b = jnp.concatenate([grad_b[:, :half], grad_b[:, half:]], 0)
    lead, front = group == 0, mp == 0
    grad_a = jnp.concatenate(
        [jnp.where(front, grad_kept, grad_taken), jnp.where(front, grad_taken, grad_kept)], 0
    )
    mine = jnp.where(lead, grad_a, grad_b)
    given_part = jnp.where(lead, grad_b, grad_a).astype(jnp.bfloat16)
    mine = mine + swap_cores(given_part).astype(jnp.float32)
    total = add_over_chips(mine)
    passed = swap_cores(total)
    total_a = jnp.where(lead, total, passed)
    total_b = jnp.where(lead, passed, total)
    rank = adapter_up.shape[0]
    grad_a = lax.dynamic_slice_in_dim(total_a, mp * rank, rank, 0).astype(jnp.float32).T
    grad_b = jnp.concatenate([total_b[:rank], total_b[rank:]], 1).astype(jnp.float32)
    return (grad_a, grad_b, own_scores)


def solution(mesh):
    fine = Mesh(mesh.devices.reshape(2, 4, 2, 8, 2), ("group", "x", "yl", "z", "mp"))
    dp = ("x", "yl", "z")
    rows = ("group",) + dp
    return jax.shard_map(
        shards,
        mesh=fine,
        in_specs=(
            P(rows, "mp"),
            P(rows + ("mp",), None),
            P("mp", dp),
            P("mp", None),
            P(),
            P(),
            P(),
            P(),
            P(),
            P(),
            P(rows + ("mp",), None),
            P(),
            P(),
            P(),
            P(),
            P(dp, None, None),
            P(rows + ("mp",), None),
            P(rows + ("mp",), None),
        ),
        out_specs=(P("mp", None), P(), P(rows + ("mp",))),
        check_vma=False,
    )
```

```python
import jax
import jax.numpy as jnp
from jax import lax
from jax.experimental import pallas as pl
from jax.experimental.pallas import tpu as pltpu
from jax.sharding import Mesh
from jax.sharding import PartitionSpec as P

TILE = 8


epsilon = 1e-06
sigma_last = 0.7
loss_weight = 16.0


def product(left, right):
    return jnp.dot(left, right, preferred_element_type=jnp.float32)


def product_final(left, right):
    return lax.dot_general(
        left, right, (((1,), (1,)), ((), ())), preferred_element_type=jnp.float32
    )


def normalize(values):
    centre = values - jnp.mean(values, -1, keepdims=True)
    inverse_std = lax.rsqrt(jnp.mean(centre * centre, -1, keepdims=True) + epsilon)
    return (centre * inverse_std, inverse_std)


def norm_back(grad_normed, normed, inverse_std):
    grad_mean = jnp.mean(grad_normed, -1, keepdims=True)
    cross_mean = jnp.mean(grad_normed * normed, -1, keepdims=True)
    return (grad_normed - grad_mean - normed * cross_mean) * inverse_std


def crop_score(query, text):
    text_wide = text.astype(jnp.float32)
    width = query.shape[-1]
    query_rms = jnp.sqrt(jnp.mean(query * query, -1, keepdims=True) + epsilon)
    text_rms = jnp.sqrt(jnp.mean(text_wide * text_wide, -1, keepdims=True) + epsilon)
    scores = jnp.mean(query * text_wide, -1, keepdims=True) / (query_rms * text_rms)
    grad_query = -loss_weight * (
        text_wide / (width * query_rms * text_rms)
        - scores * query / (width * query_rms * query_rms)
    )
    return (scores[:, 0], grad_query.astype(jnp.bfloat16))


PLANE = ("x", "yl", "mp")
DP = ("x", "yl", "z")


def shift(block, axis, size, step):
    return lax.ppermute(block, axis, [(i, (i + step) % size) for i in range(size)])


def ring(block, axis, size):
    held = [(0, block)]
    up = down = block
    for step in range(1, size // 2):
        up, down = shift(up, axis, size, 1), shift(down, axis, size, -1)
        held += [(-step, up), (step, down)]
    half = block.shape[0] // 2
    if half == 0 or block.shape[0] % 2:
        held.append((size // 2, shift(up, axis, size, 1)))
    else:
        first = shift(up[:half], axis, size, 1)
        second = shift(down[half:], axis, size, -1)
        held.append((size // 2, jnp.concatenate([first, second], 0)))
    return held


def place(blocks, axis, size):
    own = lax.axis_index(axis)
    shape = blocks[0][1].shape
    filled = jnp.zeros((size,) + shape, blocks[0][1].dtype)
    for offset, block in blocks:
        filled = lax.dynamic_update_index_in_dim(filled, block, (own + offset + size) % size, 0)
    return filled


def swap_cores(block):
    return lax.ppermute(block, "group", [(0, 1), (1, 0)])


def gather_weight(shard, given, down):
    picked = lax.ppermute(shard, ("group", "mp"), [(0, 0), (2, 1), (1, 2), (3, 3)])
    beside = shift(picked, "yl", 2, 1)
    pair = jnp.where(
        lax.axis_index("yl") == 0, jnp.stack([picked, beside]), jnp.stack([beside, picked])
    )
    columns, width = shard.shape
    down_taken = shift(down, "mp", 2, 1)
    given, down_taken, _ = lax.optimization_barrier((given, down_taken, pair))
    taken = shift(given, "mp", 2, 1)
    along_z = place(ring(pair, "z", 8), "z", 8)
    half = 8 * columns
    front, rear = along_z[:, 0].reshape(half, width), along_z[:, 1].reshape(half, width)
    up_front, down_rear = shift(front, "x", 4, 1), shift(rear, "x", 4, -1)
    front_later, rear_later, taken = lax.optimization_barrier((front, rear, taken))
    up_rear, down_front = shift(rear_later, "x", 4, 1), shift(front_later, "x", 4, -1)
    return taken, down_taken, (front, rear, up_front, down_rear, up_rear, down_front)


def finish_weight(held, ready):
    front, rear, up_front, down_rear, up_rear, down_front = held
    far_front, far_rear = shift(up_front, "x", 4, 1), shift(down_rear, "x", 4, -1)
    own, half = lax.axis_index("x"), front.shape[0]
    held, rows = [], []
    for offset, first, part in (
        (0, 0, front),
        (0, half, rear),
        (-1, 0, up_front),
        (1, half, down_rear),
        (-1, half, up_rear),
        (1, 0, down_front),
        (2, 0, far_front),
        (2, half, far_rear),
    ):
        held.append(part)
        rows.append(jnp.bitwise_and(own + offset + 4, 3) * 2 * half + first)
    *waited, ready = lax.optimization_barrier((*held[:5], ready))
    other = [swap_cores(part) for part in waited + held[5:]]
    return held + other, jnp.stack(rows).astype(jnp.int32), ready


def pad_row(vector, width):
    return jnp.pad(vector.astype(jnp.float32), (0, width - vector.shape[0]))


PARTS = 8
ROWS = 512
PARTS_SPACE = pltpu.HBM


def product_first(left, right):
    return lax.dot_general(
        left, right, (((0,), (0,)), ((), ())), preferred_element_type=jnp.float32
    )


def by_columns(array):
    return pl.BlockSpec((array.shape[0], ROWS), lambda i: (0, i))


def forward_kernel(
    place_ref,
    kept_ref,
    taken_ref,
    down_kept,
    down_taken,
    up_ref,
    resid_ref,
    rows_ref,
    velocity_ref,
    noised_ref,
    decoder_ref,
    embed_ref,
    select_ref,
    *rest,
):
    parts = rest[: 2 * PARTS]
    lowrank_ref, normed_ref, stats_ref, decoded_ref, crop_ref, packed_ref = rest[
        2 * PARTS : 2 * PARTS + 6
    ]
    weight, stream, half_sum, resid_held, embed_held, modulated, pooled, sems = rest[2 * PARTS + 6 :]
    step = pl.program_id(0)
    height = parts[0].shape[0]
    copies = []
    for i, part in enumerate(parts):
        row = pl.multiple_of(place_ref[i % PARTS], 16)
        copies.append(
            pltpu.make_async_copy(part, weight.at[i // PARTS, pl.ds(row, height)], sems.at[i])
        )

    copies.append(pltpu.make_async_copy(resid_ref, resid_held, sems.at[2 * PARTS]))
    copies.append(pltpu.make_async_copy(embed_ref, embed_held, sems.at[2 * PARTS + 1]))
    for copy in copies:
        copy.start()

    kept, taken = kept_ref[...], taken_ref[...]
    lowrank = product(down_kept[...], kept) + product(down_taken[...], taken)
    high = lowrank.astype(jnp.bfloat16)
    low = (lowrank - high.astype(jnp.float32)).astype(jnp.bfloat16)
    lowrank_ref[...] = high
    both = jnp.concatenate([high, low], 1)
    straight = place_ref[PARTS] == 0
    near, far = jnp.where(straight, kept, taken), jnp.where(straight, taken, kept)

    width = stream.shape[1]
    view, pix, latent_width = embed_ref.shape[1], embed_ref.shape[0], velocity_ref.shape[0]
    for copy in copies[:PARTS]:
        copy.wait()
    half_sum[...] = product(weight[0], near)
    for copy in copies[PARTS:]:
        copy.wait()
    for first in range(0, width, 384):
        columns = slice(first, min(first + 384, width))
        adapted = product_first(up_ref[:, columns], both)
        projected = (
            half_sum[columns, :]
            + product(weight[1, columns], far)
            + (adapted[:, :ROWS] + adapted[:, ROWS:])
        ).T
        stream[:, columns] = (
            resid_held[:, columns].astype(jnp.float32) + rows_ref[0:1, columns] * projected
        )
    count = 64
    for first in range(0, ROWS, count):
        rows = slice(first, first + count)
        normed, inverse_std = normalize(stream[rows, :])
        normed_ref[rows, :] = normed.astype(jnp.bfloat16)
        stats_ref[rows, 0:1] = inverse_std
        modulated[rows, :] = (normed * (1.0 + rows_ref[1:2, :]) + rows_ref[2:3, :]).astype(
            jnp.bfloat16
        )
    velocity = product_final(modulated[...], velocity_ref[...]) + rows_ref[3:4, :latent_width]
    latent = noised_ref[...].astype(jnp.float32).T - sigma_last * velocity
    inner = product(latent.astype(jnp.bfloat16), decoder_ref[...]) + rows_ref[4:5, :pix]
    decoded = jnp.tanh(inner)
    decoded_ref[...] = decoded
    embedded = product(decoded.astype(jnp.bfloat16), embed_held[...])
    crop_normed, crop_inverse = normalize(embedded)
    crop_ref[...] = crop_normed.astype(jnp.bfloat16)
    stats_ref[:, 1:2] = crop_inverse
    crops = ROWS // TILE
    scaled = (crop_normed * rows_ref[5:6, :view]).reshape(crops, TILE, view)
    pooled[pl.ds(pl.multiple_of(step * crops, crops), crops), :] = jnp.mean(scaled, 1).astype(
        jnp.bfloat16
    )

    @pl.when(step == pl.num_programs(0) - 1)
    def _():
        packed_ref[...] = product(select_ref[...], pooled[...]).astype(jnp.bfloat16)


def whole(array):
    return pl.BlockSpec(array.shape, lambda i: (0,) * array.ndim)


def by_rows(array):
    return pl.BlockSpec((ROWS, array.shape[1]), lambda i: (i, 0))


def forward_call(place_rows, heads, downs, up, resid, vectors, velocity_t, noised_t, decoder, embed, select, parts, interpret=False):
    count, width = resid.shape
    rank, view, pix = up.shape[0], embed.shape[1], embed.shape[0]
    shape = jax.ShapeDtypeStruct
    outs = (
        shape((rank, count), jnp.bfloat16),
        shape((count, width), jnp.bfloat16),
        shape((count, 128), jnp.float32),
        shape((count, pix), jnp.float32),
        shape((count, view), jnp.bfloat16),
        shape((select.shape[0], view), jnp.bfloat16),
    )
    return pl.pallas_call(
        forward_kernel,
        grid=(count // ROWS,),
        in_specs=[pl.BlockSpec(memory_space=pltpu.SMEM)]
        + [by_columns(heads[0])] * 2
        + [whole(downs[0])] * 2
        + [whole(up), pl.BlockSpec(memory_space=PARTS_SPACE), whole(vectors), whole(velocity_t)]
        + [by_columns(noised_t), whole(decoder), pl.BlockSpec(memory_space=PARTS_SPACE)]
        + [whole(select)]
        + [pl.BlockSpec(memory_space=PARTS_SPACE)] * len(parts),
        out_specs=[by_columns(outs[0])] + [by_rows(a) for a in outs[1:5]] + [whole(outs[5])],
        out_shape=outs,
        scratch_shapes=[
            pltpu.VMEM((2, width, heads[0].shape[0]), jnp.bfloat16),
            pltpu.VMEM((ROWS, width), jnp.float32),
            pltpu.VMEM((width, ROWS), jnp.float32),
            pltpu.VMEM(resid.shape, jnp.bfloat16),
            pltpu.VMEM(embed.shape, jnp.bfloat16),
            pltpu.VMEM((ROWS, width), jnp.bfloat16),
            pltpu.VMEM((count // TILE, view), jnp.bfloat16),
            pltpu.SemaphoreType.DMA((2 * PARTS + 2,)),
        ],
        compiler_params=pltpu.CompilerParams(vmem_limit_bytes=58 * 1024 * 1024),
        name="forward",
        interpret=interpret,
    )(place_rows, *heads, *downs, up, resid, vectors, velocity_t, noised_t, decoder, embed, select, *parts)


def backward_kernel(
    back_ref,
    pick_ref,
    crop_hbm,
    stats_ref,
    rows_ref,
    embed_hbm,
    decoded_hbm,
    decoder_ref,
    velocity_ref,
    normed_hbm,
    up_ref,
    lowrank_ref,
    kept_hbm,
    taken_hbm,
    grad_kept,
    grad_taken,
    grad_b,
    score_ref,
    output,
    crop_ref,
    embed_ref,
    decoded_ref,
    normed_ref,
    kept_ref,
    taken_ref,
    sems,
):
    step = pl.program_id(0)
    copies = [
        pltpu.make_async_copy(source, target, sems.at[i])
        for i, (source, target) in enumerate(
            (
                (crop_hbm, crop_ref),
                (embed_hbm, embed_ref),
                (decoded_hbm, decoded_ref),
                (normed_hbm, normed_ref),
                (kept_hbm, kept_ref),
                (taken_hbm, taken_ref),
            )
        )
    ]
    for copy in copies:
        copy.start()
    view = embed_ref.shape[1]
    crops = ROWS // TILE
    back = jnp.dot(pick_ref[...], back_ref[...], preferred_element_type=jnp.float32)
    score_ref[...] = back[:, view:]
    spread = jnp.broadcast_to((back[:, :view] / TILE)[:, None, :], (crops, TILE, view))
    spread = spread.reshape(ROWS, view) * rows_ref[5:6, :view]
    copies[0].wait()
    grad_embedded = norm_back(
        spread, crop_ref[...].astype(jnp.float32), stats_ref[:, 1:2]
    ).astype(jnp.bfloat16)
    copies[1].wait()
    pixel_grad = product_final(grad_embedded, embed_ref[...]).astype(jnp.bfloat16)
    copies[2].wait()
    decoded = decoded_ref[...]
    grad_inner = (pixel_grad.astype(jnp.float32) * (1.0 - decoded * decoded)).astype(jnp.bfloat16)
    grad_velocity = (-sigma_last * product_final(grad_inner, decoder_ref[...])).astype(jnp.bfloat16)
    copies[3].wait()
    count = 64
    for first in range(0, ROWS, count):
        rows = slice(first, first + count)
        grad_modulated = jnp.dot(
            grad_velocity[rows, :], velocity_ref[...], preferred_element_type=jnp.float32
        )
        grad_stream = norm_back(
            grad_modulated * (1.0 + rows_ref[1:2, :]),
            normed_ref[rows, :].astype(jnp.float32),
            stats_ref[rows, 0:1],
        )
        output[rows, :] = (rows_ref[0:1, :] * grad_stream).astype(jnp.bfloat16)
    rank_grad = product_final(up_ref[...], output[...]).astype(jnp.bfloat16)
    copies[4].wait()
    copies[5].wait()
    kept = product_final(rank_grad, kept_ref[...])
    taken = product_final(rank_grad, taken_ref[...])
    up_part = jnp.dot(lowrank_ref[...], output[...], preferred_element_type=jnp.float32)

    @pl.when(step == 0)
    def _():
        grad_kept[...] = kept
        grad_taken[...] = taken
        grad_b[...] = up_part

    @pl.when(step > 0)
    def _():
        grad_kept[...] += kept
        grad_taken[...] += taken
        grad_b[...] += up_part


def backward_call(back, pick, crop_normed, stats, vectors, embed, decoded, decoder, velocity_t, normed, up, lowrank_t, heads, interpret=False):
    count, width = normed.shape
    rank, half = up.shape[0], heads[0].shape[0]
    shape = jax.ShapeDtypeStruct
    crops = ROWS // TILE
    outs = (
        shape((rank, half), jnp.float32),
        shape((rank, half), jnp.float32),
        shape((rank, width), jnp.float32),
        shape((count // TILE, 128), jnp.float32),
    )
    return pl.pallas_call(
        backward_kernel,
        grid=(count // ROWS,),
        in_specs=[
            whole(back),
            pl.BlockSpec((crops, pick.shape[1]), lambda i: (i, 0)),
            pl.BlockSpec(memory_space=PARTS_SPACE),
            by_rows(stats),
            whole(vectors),
            pl.BlockSpec(memory_space=PARTS_SPACE),
            pl.BlockSpec(memory_space=PARTS_SPACE),
            whole(decoder),
            whole(velocity_t),
            pl.BlockSpec(memory_space=PARTS_SPACE),
            whole(up),
            pl.BlockSpec((rank, ROWS), lambda i: (0, i)),
            pl.BlockSpec(memory_space=PARTS_SPACE),
            pl.BlockSpec(memory_space=PARTS_SPACE),
        ],
        out_specs=[whole(a) for a in outs[:3]] + [pl.BlockSpec((crops, 128), lambda i: (i, 0))],
        out_shape=outs,
        scratch_shapes=[pltpu.VMEM((ROWS, width), jnp.bfloat16)]
        + [
            pltpu.VMEM(a.shape, a.dtype)
            for a in (crop_normed, embed, decoded, normed, heads[0], heads[1])
        ]
        + [pltpu.SemaphoreType.DMA((6,))],
        compiler_params=pltpu.CompilerParams(vmem_limit_bytes=58 * 1024 * 1024),
        name="backward",
        interpret=interpret,
    )(back, pick, crop_normed, stats, vectors, embed, decoded, decoder, velocity_t, normed, up, lowrank_t, *heads)


def exchange(pieces, axes):
    return lax.all_to_all(pieces, axes, split_axis=0, concat_axis=0, tiled=True)


def add_over_chips(part):
    width = part.shape[1]
    held = exchange(part.astype(jnp.bfloat16).reshape(16, 8, width), PLANE)
    share = jnp.sum(held.astype(jnp.float32), 0, keepdims=True).astype(jnp.bfloat16)
    held = exchange(jnp.broadcast_to(share, (8, 8, width)), "z")
    share = jnp.sum(held.astype(jnp.float32), 0, keepdims=True).astype(jnp.bfloat16)
    held = exchange(jnp.broadcast_to(share, (16, 8, width)), PLANE)
    return held.reshape(128, width)


def shards(
    attention_result,
    resid,
    attention_output_weight,
    adapter_down,
    adapter_up,
    branch_gate,
    final_norm_scale,
    final_norm_shift,
    velocity_weight,
    velocity_bias,
    noised_latent_tokens,
    decoder_weight,
    decoder_bias,
    patch_embed_weight,
    reward_norm_gain,
    reward_head_bank,
    prompt_features,
    assignment,
):
    group, mp = lax.axis_index("group"), lax.axis_index("mp")
    row_count, width = resid.shape
    half = width // 2
    tiles_dev = row_count // TILE
    heads_t = attention_result.T
    kept = lax.dynamic_slice_in_dim(heads_t, mp * row_count, row_count, 1)
    given = lax.dynamic_slice_in_dim(heads_t, (1 - mp) * row_count, row_count, 1)
    taken, down_taken, held = gather_weight(attention_output_weight.T, given, adapter_down.T)

    _, small, prompts, names = lax.optimization_barrier(
        (
            held[2],
            (
                branch_gate,
                final_norm_scale,
                final_norm_shift,
                velocity_bias,
                decoder_bias,
                reward_norm_gain,
            ),
            prompt_features,
            assignment,
        )
    )

    dp_count = 64
    capacity = 2
    target = names[:, 0]
    earlier = jnp.arange(tiles_dev)[None, :] < jnp.arange(tiles_dev)[:, None]
    matches = jnp.logical_and(target[:, None] == target[None, :], earlier)
    slot_index = jnp.sum(matches.astype(jnp.int32), 1)
    position = target * capacity + slot_index
    select = (
        jnp.arange(dp_count * capacity, dtype=jnp.int32)[:, None] == position[None, :]
    ).astype(jnp.bfloat16)
    texts = jnp.dot(select, prompts, preferred_element_type=jnp.float32)
    texts = texts.astype(jnp.bfloat16).reshape(dp_count, capacity, prompt_features.shape[1])
    vectors = jnp.stack([pad_row(vector, width) for vector in small])
    pick = select.T
    crop_texts = lax.all_to_all(texts, DP, split_axis=0, concat_axis=0, tiled=True)
    parts, part_rows, (crop_texts, vectors, select, pick) = finish_weight(
        held, (crop_texts, vectors, select, pick)
    )

    same = group == mp
    heads = (kept, taken)
    downs = (adapter_down.T, down_taken)
    pairing = jnp.where(same, 0, 1).astype(jnp.int32)[None]

    velocity_t = velocity_weight.T
    lowrank_t, normed, stats, decoded, crop_normed, packed = forward_call(
        jnp.concatenate([part_rows, pairing]),
        heads,
        downs,
        adapter_up,
        resid,
        vectors,
        velocity_t,
        noised_latent_tokens.T,
        decoder_weight,
        patch_embed_weight,
        select,
        parts,
    )
    width_view = packed.shape[1]
    own_head = reward_head_bank[0]
    crop_pooled = lax.all_to_all(
        packed.reshape(dp_count, capacity, width_view), DP, split_axis=0, concat_axis=0, tiled=True
    ).reshape(dp_count * capacity, width_view)
    query = jnp.dot(crop_pooled, own_head, preferred_element_type=jnp.float32)
    scores, grad_query = crop_score(query, crop_texts.reshape(dp_count * capacity, -1))
    grad_pooled = product_final(grad_query, own_head).astype(jnp.bfloat16)
    back = jnp.concatenate(
        [grad_pooled, jnp.broadcast_to(scores.astype(jnp.bfloat16)[:, None], (dp_count * capacity, 128))],
        1,
    )
    back = lax.all_to_all(
        back.reshape(dp_count, capacity, width_view + 128), DP, split_axis=0, concat_axis=0, tiled=True
    ).reshape(dp_count * capacity, width_view + 128)
    grad_kept, grad_taken, grad_b, scores_wide = backward_call(
        back,
        pick,
        crop_normed,
        stats,
        vectors,
        patch_embed_weight,
        decoded,
        decoder_weight,
        velocity_t,
        normed,
        adapter_up,
        lowrank_t,
        heads,
    )
    own_scores = scores_wide[:, 0].astype(jnp.bfloat16)
    grad_b = jnp.concatenate([grad_b[:, :half], grad_b[:, half:]], 0)
    lead, front = group == 0, mp == 0
    grad_a = jnp.concatenate(
        [jnp.where(front, grad_kept, grad_taken), jnp.where(front, grad_taken, grad_kept)], 0
    )
    mine = jnp.where(lead, grad_a, grad_b)
    given_part = jnp.where(lead, grad_b, grad_a).astype(jnp.bfloat16)
    mine = mine + swap_cores(given_part).astype(jnp.float32)
    total = add_over_chips(mine)
    passed = swap_cores(total)
    total_a = jnp.where(lead, total, passed)
    total_b = jnp.where(lead, passed, total)
    rank = adapter_up.shape[0]
    grad_a = lax.dynamic_slice_in_dim(total_a, mp * rank, rank, 0).astype(jnp.float32).T
    grad_b = jnp.concatenate([total_b[:rank], total_b[rank:]], 1).astype(jnp.float32)
    return (grad_a, grad_b, own_scores)


def solution(mesh):
    fine = Mesh(mesh.devices.reshape(2, 4, 2, 8, 2), ("group", "x", "yl", "z", "mp"))
    dp = ("x", "yl", "z")
    rows = ("group",) + dp
    return jax.shard_map(
        shards,
        mesh=fine,
        in_specs=(
            P(rows, "mp"),
            P(rows + ("mp",), None),
            P("mp", dp),
            P("mp", None),
            P(),
            P(),
            P(),
            P(),
            P(),
            P(),
            P(rows + ("mp",), None),
            P(),
            P(),
            P(),
            P(),
            P(dp, None, None),
            P(rows + ("mp",), None),
            P(rows + ("mp",), None),
        ),
        out_specs=(P("mp", None), P(), P(rows + ("mp",))),
        check_vma=False,
    )
```

```python
import jax
import jax.numpy as jnp
from jax import lax
from jax.experimental import pallas as pl
from jax.experimental.pallas import tpu as pltpu
from jax.sharding import Mesh
from jax.sharding import PartitionSpec as P

TILE = 8


epsilon = 1e-06
sigma_last = 0.7
loss_weight = 16.0


def product(left, right):
    return jnp.dot(left, right, preferred_element_type=jnp.float32)


def product_final(left, right):
    return lax.dot_general(
        left, right, (((1,), (1,)), ((), ())), preferred_element_type=jnp.float32
    )


def normalize(values):
    centre = values - jnp.mean(values, -1, keepdims=True)
    inverse_std = lax.rsqrt(jnp.mean(centre * centre, -1, keepdims=True) + epsilon)
    return (centre * inverse_std, inverse_std)


def norm_back(grad_normed, normed, inverse_std):
    grad_mean = jnp.mean(grad_normed, -1, keepdims=True)
    cross_mean = jnp.mean(grad_normed * normed, -1, keepdims=True)
    return (grad_normed - grad_mean - normed * cross_mean) * inverse_std


def crop_score(query, text):
    text_wide = text.astype(jnp.float32)
    width = query.shape[-1]
    query_rms = jnp.sqrt(jnp.mean(query * query, -1, keepdims=True) + epsilon)
    text_rms = jnp.sqrt(jnp.mean(text_wide * text_wide, -1, keepdims=True) + epsilon)
    scores = jnp.mean(query * text_wide, -1, keepdims=True) / (query_rms * text_rms)
    grad_query = -loss_weight * (
        text_wide / (width * query_rms * text_rms)
        - scores * query / (width * query_rms * query_rms)
    )
    return (scores[:, 0], grad_query.astype(jnp.bfloat16))


PLANE = ("x", "yl", "mp")
DP = ("x", "yl", "z")


def shift(block, axis, size, step):
    return lax.ppermute(block, axis, [(i, (i + step) % size) for i in range(size)])


def ring(block, axis, size):
    held = [(0, block)]
    up = down = block
    for step in range(1, size // 2):
        up, down = shift(up, axis, size, 1), shift(down, axis, size, -1)
        held += [(-step, up), (step, down)]
    half = block.shape[0] // 2
    if half == 0 or block.shape[0] % 2:
        held.append((size // 2, shift(up, axis, size, 1)))
    else:
        first = shift(up[:half], axis, size, 1)
        second = shift(down[half:], axis, size, -1)
        held.append((size // 2, jnp.concatenate([first, second], 0)))
    return held


def place(blocks, axis, size):
    own = lax.axis_index(axis)
    shape = blocks[0][1].shape
    filled = jnp.zeros((size,) + shape, blocks[0][1].dtype)
    for offset, block in blocks:
        filled = lax.dynamic_update_index_in_dim(filled, block, (own + offset + size) % size, 0)
    return filled


def swap_cores(block):
    return lax.ppermute(block, "group", [(0, 1), (1, 0)])


def gather_weight(shard, given, down):
    picked = lax.ppermute(shard, ("group", "mp"), [(0, 0), (2, 1), (1, 2), (3, 3)])
    routes = [(a * 4 + b * 2 + c, c * 4 + (1 - b) * 2 + a) for a in (0, 1) for b in (0, 1) for c in (0, 1)]
    beside = lax.ppermute(shard, ("group", "yl", "mp"), routes)
    pair = jnp.where(
        lax.axis_index("yl") == 0, jnp.stack([picked, beside]), jnp.stack([beside, picked])
    )
    columns, width = shard.shape
    down_taken = shift(down, "mp", 2, 1)
    given, down_taken, _ = lax.optimization_barrier((given, down_taken, pair))
    taken = shift(given, "mp", 2, 1)
    along_z = place(ring(pair, "z", 8), "z", 8)
    half = 8 * columns
    front, rear = along_z[:, 0].reshape(half, width), along_z[:, 1].reshape(half, width)
    up_front, down_rear = shift(front, "x", 4, 1), shift(rear, "x", 4, -1)
    front_later, rear_later, taken = lax.optimization_barrier((front, rear, taken))
    up_rear, down_front = shift(rear_later, "x", 4, 1), shift(front_later, "x", 4, -1)
    return taken, down_taken, (front, rear, up_front, down_rear, up_rear, down_front)


def finish_weight(held, ready):
    front, rear, up_front, down_rear, up_rear, down_front = held
    far_front, far_rear = shift(up_front, "x", 4, 1), shift(down_rear, "x", 4, -1)
    own, half = lax.axis_index("x"), front.shape[0]
    held, rows = [], []
    for offset, first, part in (
        (0, 0, front),
        (0, half, rear),
        (-1, 0, up_front),
        (1, half, down_rear),
        (-1, half, up_rear),
        (1, 0, down_front),
        (2, 0, far_front),
        (2, half, far_rear),
    ):
        held.append(part)
        rows.append(jnp.bitwise_and(own + offset + 4, 3) * 2 * half + first)
    *waited, ready = lax.optimization_barrier((*held[:5], ready))
    other = [swap_cores(part) for part in waited + held[5:]]
    return held + other, jnp.stack(rows).astype(jnp.int32), ready


def pad_row(vector, width):
    return jnp.pad(vector.astype(jnp.float32), (0, width - vector.shape[0]))


PARTS = 8
ROWS = 512
PARTS_SPACE = pltpu.HBM


def product_first(left, right):
    return lax.dot_general(
        left, right, (((0,), (0,)), ((), ())), preferred_element_type=jnp.float32
    )


def by_columns(array):
    return pl.BlockSpec((array.shape[0], ROWS), lambda i: (0, i))


def forward_kernel(
    place_ref,
    kept_ref,
    taken_ref,
    down_kept,
    down_taken,
    up_ref,
    resid_ref,
    rows_ref,
    velocity_ref,
    noised_ref,
    decoder_ref,
    embed_ref,
    select_ref,
    *rest,
):
    parts = rest[: 2 * PARTS]
    lowrank_ref, normed_ref, stats_ref, decoded_ref, crop_ref, packed_ref = rest[
        2 * PARTS : 2 * PARTS + 6
    ]
    weight, stream, half_sum, resid_held, embed_held, modulated, pooled, sems = rest[2 * PARTS + 6 :]
    step = pl.program_id(0)
    height = parts[0].shape[0]
    copies = []
    for i, part in enumerate(parts):
        row = pl.multiple_of(place_ref[i % PARTS], 16)
        copies.append(
            pltpu.make_async_copy(part, weight.at[i // PARTS, pl.ds(row, height)], sems.at[i])
        )

    copies.append(pltpu.make_async_copy(resid_ref, resid_held, sems.at[2 * PARTS]))
    copies.append(pltpu.make_async_copy(embed_ref, embed_held, sems.at[2 * PARTS + 1]))
    for copy in copies:
        copy.start()

    kept, taken = kept_ref[...], taken_ref[...]
    lowrank = product(down_kept[...], kept) + product(down_taken[...], taken)
    high = lowrank.astype(jnp.bfloat16)
    low = (lowrank - high.astype(jnp.float32)).astype(jnp.bfloat16)
    lowrank_ref[...] = high
    both = jnp.concatenate([high, low], 1)
    straight = place_ref[PARTS] == 0
    near, far = jnp.where(straight, kept, taken), jnp.where(straight, taken, kept)

    width = stream.shape[1]
    view, pix, latent_width = embed_ref.shape[1], embed_ref.shape[0], velocity_ref.shape[0]
    for copy in copies[:PARTS]:
        copy.wait()
    half_sum[...] = product(weight[0], near)
    for copy in copies[PARTS:]:
        copy.wait()
    for first in range(0, width, 384):
        columns = slice(first, min(first + 384, width))
        adapted = product_first(up_ref[:, columns], both)
        projected = (
            half_sum[columns, :]
            + product(weight[1, columns], far)
            + (adapted[:, :ROWS] + adapted[:, ROWS:])
        ).T
        stream[:, columns] = (
            resid_held[:, columns].astype(jnp.float32) + rows_ref[0:1, columns] * projected
        )
    count = 64
    for first in range(0, ROWS, count):
        rows = slice(first, first + count)
        normed, inverse_std = normalize(stream[rows, :])
        normed_ref[rows, :] = normed.astype(jnp.bfloat16)
        stats_ref[rows, 0:1] = inverse_std
        modulated[rows, :] = (normed * (1.0 + rows_ref[1:2, :]) + rows_ref[2:3, :]).astype(
            jnp.bfloat16
        )
    velocity = product_final(modulated[...], velocity_ref[...]) + rows_ref[3:4, :latent_width]
    latent = noised_ref[...].astype(jnp.float32).T - sigma_last * velocity
    inner = product(latent.astype(jnp.bfloat16), decoder_ref[...]) + rows_ref[4:5, :pix]
    decoded = jnp.tanh(inner)
    decoded_ref[...] = decoded
    embedded = product(decoded.astype(jnp.bfloat16), embed_held[...])
    crop_normed, crop_inverse = normalize(embedded)
    crop_ref[...] = crop_normed.astype(jnp.bfloat16)
    stats_ref[:, 1:2] = crop_inverse
    crops = ROWS // TILE
    scaled = (crop_normed * rows_ref[5:6, :view]).reshape(crops, TILE, view)
    pooled[pl.ds(pl.multiple_of(step * crops, crops), crops), :] = jnp.mean(scaled, 1).astype(
        jnp.bfloat16
    )

    @pl.when(step == pl.num_programs(0) - 1)
    def _():
        packed_ref[...] = product(select_ref[...], pooled[...]).astype(jnp.bfloat16)


def whole(array):
    return pl.BlockSpec(array.shape, lambda i: (0,) * array.ndim)


def by_rows(array):
    return pl.BlockSpec((ROWS, array.shape[1]), lambda i: (i, 0))


def forward_call(place_rows, heads, downs, up, resid, vectors, velocity_t, noised_t, decoder, embed, select, parts, interpret=False):
    count, width = resid.shape
    rank, view, pix = up.shape[0], embed.shape[1], embed.shape[0]
    shape = jax.ShapeDtypeStruct
    outs = (
        shape((rank, count), jnp.bfloat16),
        shape((count, width), jnp.bfloat16),
        shape((count, 128), jnp.float32),
        shape((count, pix), jnp.float32),
        shape((count, view), jnp.bfloat16),
        shape((select.shape[0], view), jnp.bfloat16),
    )
    return pl.pallas_call(
        forward_kernel,
        grid=(count // ROWS,),
        in_specs=[pl.BlockSpec(memory_space=pltpu.SMEM)]
        + [by_columns(heads[0])] * 2
        + [whole(downs[0])] * 2
        + [whole(up), pl.BlockSpec(memory_space=PARTS_SPACE), whole(vectors), whole(velocity_t)]
        + [by_columns(noised_t), whole(decoder), pl.BlockSpec(memory_space=PARTS_SPACE)]
        + [whole(select)]
        + [pl.BlockSpec(memory_space=PARTS_SPACE)] * len(parts),
        out_specs=[by_columns(outs[0])] + [by_rows(a) for a in outs[1:5]] + [whole(outs[5])],
        out_shape=outs,
        scratch_shapes=[
            pltpu.VMEM((2, width, heads[0].shape[0]), jnp.bfloat16),
            pltpu.VMEM((ROWS, width), jnp.float32),
            pltpu.VMEM((width, ROWS), jnp.float32),
            pltpu.VMEM(resid.shape, jnp.bfloat16),
            pltpu.VMEM(embed.shape, jnp.bfloat16),
            pltpu.VMEM((ROWS, width), jnp.bfloat16),
            pltpu.VMEM((count // TILE, view), jnp.bfloat16),
            pltpu.SemaphoreType.DMA((2 * PARTS + 2,)),
        ],
        compiler_params=pltpu.CompilerParams(vmem_limit_bytes=58 * 1024 * 1024),
        name="forward",
        interpret=interpret,
    )(place_rows, *heads, *downs, up, resid, vectors, velocity_t, noised_t, decoder, embed, select, *parts)


def backward_kernel(
    back_ref,
    pick_ref,
    crop_hbm,
    stats_ref,
    rows_ref,
    embed_hbm,
    decoded_hbm,
    decoder_ref,
    velocity_ref,
    normed_hbm,
    up_ref,
    lowrank_ref,
    kept_hbm,
    taken_hbm,
    grad_kept,
    grad_taken,
    grad_b,
    score_ref,
    output,
    crop_ref,
    embed_ref,
    decoded_ref,
    normed_ref,
    kept_ref,
    taken_ref,
    sems,
):
    step = pl.program_id(0)
    copies = [
        pltpu.make_async_copy(source, target, sems.at[i])
        for i, (source, target) in enumerate(
            (
                (crop_hbm, crop_ref),
                (embed_hbm, embed_ref),
                (decoded_hbm, decoded_ref),
                (normed_hbm, normed_ref),
                (kept_hbm, kept_ref),
                (taken_hbm, taken_ref),
            )
        )
    ]
    for copy in copies:
        copy.start()
    view = embed_ref.shape[1]
    crops = ROWS // TILE
    back = jnp.dot(pick_ref[...], back_ref[...], preferred_element_type=jnp.float32)
    score_ref[...] = back[:, view:]
    spread = jnp.broadcast_to((back[:, :view] / TILE)[:, None, :], (crops, TILE, view))
    spread = spread.reshape(ROWS, view) * rows_ref[5:6, :view]
    copies[0].wait()
    grad_embedded = norm_back(
        spread, crop_ref[...].astype(jnp.float32), stats_ref[:, 1:2]
    ).astype(jnp.bfloat16)
    copies[1].wait()
    pixel_grad = product_final(grad_embedded, embed_ref[...]).astype(jnp.bfloat16)
    copies[2].wait()
    decoded = decoded_ref[...]
    grad_inner = (pixel_grad.astype(jnp.float32) * (1.0 - decoded * decoded)).astype(jnp.bfloat16)
    grad_velocity = (-sigma_last * product_final(grad_inner, decoder_ref[...])).astype(jnp.bfloat16)
    copies[3].wait()
    count = 64
    for first in range(0, ROWS, count):
        rows = slice(first, first + count)
        grad_modulated = jnp.dot(
            grad_velocity[rows, :], velocity_ref[...], preferred_element_type=jnp.float32
        )
        grad_stream = norm_back(
            grad_modulated * (1.0 + rows_ref[1:2, :]),
            normed_ref[rows, :].astype(jnp.float32),
            stats_ref[rows, 0:1],
        )
        output[rows, :] = (rows_ref[0:1, :] * grad_stream).astype(jnp.bfloat16)
    rank_grad = product_final(up_ref[...], output[...]).astype(jnp.bfloat16)
    copies[4].wait()
    copies[5].wait()
    kept = product_final(rank_grad, kept_ref[...])
    taken = product_final(rank_grad, taken_ref[...])
    up_part = jnp.dot(lowrank_ref[...], output[...], preferred_element_type=jnp.float32)

    @pl.when(step == 0)
    def _():
        grad_kept[...] = kept
        grad_taken[...] = taken
        grad_b[...] = up_part

    @pl.when(step > 0)
    def _():
        grad_kept[...] += kept
        grad_taken[...] += taken
        grad_b[...] += up_part


def backward_call(back, pick, crop_normed, stats, vectors, embed, decoded, decoder, velocity_t, normed, up, lowrank_t, heads, interpret=False):
    count, width = normed.shape
    rank, half = up.shape[0], heads[0].shape[0]
    shape = jax.ShapeDtypeStruct
    crops = ROWS // TILE
    outs = (
        shape((rank, half), jnp.float32),
        shape((rank, half), jnp.float32),
        shape((rank, width), jnp.float32),
        shape((count // TILE, 128), jnp.float32),
    )
    return pl.pallas_call(
        backward_kernel,
        grid=(count // ROWS,),
        in_specs=[
            whole(back),
            pl.BlockSpec((crops, pick.shape[1]), lambda i: (i, 0)),
            pl.BlockSpec(memory_space=PARTS_SPACE),
            by_rows(stats),
            whole(vectors),
            pl.BlockSpec(memory_space=PARTS_SPACE),
            pl.BlockSpec(memory_space=PARTS_SPACE),
            whole(decoder),
            whole(velocity_t),
            pl.BlockSpec(memory_space=PARTS_SPACE),
            whole(up),
            pl.BlockSpec((rank, ROWS), lambda i: (0, i)),
            pl.BlockSpec(memory_space=PARTS_SPACE),
            pl.BlockSpec(memory_space=PARTS_SPACE),
        ],
        out_specs=[whole(a) for a in outs[:3]] + [pl.BlockSpec((crops, 128), lambda i: (i, 0))],
        out_shape=outs,
        scratch_shapes=[pltpu.VMEM((ROWS, width), jnp.bfloat16)]
        + [
            pltpu.VMEM(a.shape, a.dtype)
            for a in (crop_normed, embed, decoded, normed, heads[0], heads[1])
        ]
        + [pltpu.SemaphoreType.DMA((6,))],
        compiler_params=pltpu.CompilerParams(vmem_limit_bytes=58 * 1024 * 1024),
        name="backward",
        interpret=interpret,
    )(back, pick, crop_normed, stats, vectors, embed, decoded, decoder, velocity_t, normed, up, lowrank_t, *heads)


def exchange(pieces, axes):
    return lax.all_to_all(pieces, axes, split_axis=0, concat_axis=0, tiled=True)


def add_over_chips(part):
    width = part.shape[1]
    held = exchange(part.astype(jnp.bfloat16).reshape(16, 8, width), PLANE)
    share = jnp.sum(held.astype(jnp.float32), 0, keepdims=True).astype(jnp.bfloat16)
    held = exchange(jnp.broadcast_to(share, (8, 8, width)), "z")
    share = jnp.sum(held.astype(jnp.float32), 0, keepdims=True).astype(jnp.bfloat16)
    held = exchange(jnp.broadcast_to(share, (16, 8, width)), PLANE)
    return held.reshape(128, width)


def shards(
    attention_result,
    resid,
    attention_output_weight,
    adapter_down,
    adapter_up,
    branch_gate,
    final_norm_scale,
    final_norm_shift,
    velocity_weight,
    velocity_bias,
    noised_latent_tokens,
    decoder_weight,
    decoder_bias,
    patch_embed_weight,
    reward_norm_gain,
    reward_head_bank,
    prompt_features,
    assignment,
):
    group, mp = lax.axis_index("group"), lax.axis_index("mp")
    row_count, width = resid.shape
    half = width // 2
    tiles_dev = row_count // TILE
    heads_t = attention_result.T
    kept = lax.dynamic_slice_in_dim(heads_t, mp * row_count, row_count, 1)
    given = lax.dynamic_slice_in_dim(heads_t, (1 - mp) * row_count, row_count, 1)
    taken, down_taken, held = gather_weight(attention_output_weight.T, given, adapter_down.T)

    _, small, prompts, names = lax.optimization_barrier(
        (
            held[2],
            (
                branch_gate,
                final_norm_scale,
                final_norm_shift,
                velocity_bias,
                decoder_bias,
                reward_norm_gain,
            ),
            prompt_features,
            assignment,
        )
    )

    dp_count = 64
    capacity = 2
    target = names[:, 0]
    earlier = jnp.arange(tiles_dev)[None, :] < jnp.arange(tiles_dev)[:, None]
    matches = jnp.logical_and(target[:, None] == target[None, :], earlier)
    slot_index = jnp.sum(matches.astype(jnp.int32), 1)
    position = target * capacity + slot_index
    select = (
        jnp.arange(dp_count * capacity, dtype=jnp.int32)[:, None] == position[None, :]
    ).astype(jnp.bfloat16)
    texts = jnp.dot(select, prompts, preferred_element_type=jnp.float32)
    texts = texts.astype(jnp.bfloat16).reshape(dp_count, capacity, prompt_features.shape[1])
    vectors = jnp.stack([pad_row(vector, width) for vector in small])
    pick = select.T
    crop_texts = lax.all_to_all(texts, DP, split_axis=0, concat_axis=0, tiled=True)
    parts, part_rows, (crop_texts, vectors, select, pick) = finish_weight(
        held, (crop_texts, vectors, select, pick)
    )

    same = group == mp
    heads = (kept, taken)
    downs = (adapter_down.T, down_taken)
    pairing = jnp.where(same, 0, 1).astype(jnp.int32)[None]

    velocity_t = velocity_weight.T
    lowrank_t, normed, stats, decoded, crop_normed, packed = forward_call(
        jnp.concatenate([part_rows, pairing]),
        heads,
        downs,
        adapter_up,
        resid,
        vectors,
        velocity_t,
        noised_latent_tokens.T,
        decoder_weight,
        patch_embed_weight,
        select,
        parts,
    )
    width_view = packed.shape[1]
    own_head = reward_head_bank[0]
    crop_pooled = lax.all_to_all(
        packed.reshape(dp_count, capacity, width_view), DP, split_axis=0, concat_axis=0, tiled=True
    ).reshape(dp_count * capacity, width_view)
    query = jnp.dot(crop_pooled, own_head, preferred_element_type=jnp.float32)
    scores, grad_query = crop_score(query, crop_texts.reshape(dp_count * capacity, -1))
    grad_pooled = product_final(grad_query, own_head).astype(jnp.bfloat16)
    back = jnp.concatenate(
        [grad_pooled, jnp.broadcast_to(scores.astype(jnp.bfloat16)[:, None], (dp_count * capacity, 128))],
        1,
    )
    back = lax.all_to_all(
        back.reshape(dp_count, capacity, width_view + 128), DP, split_axis=0, concat_axis=0, tiled=True
    ).reshape(dp_count * capacity, width_view + 128)
    grad_kept, grad_taken, grad_b, scores_wide = backward_call(
        back,
        pick,
        crop_normed,
        stats,
        vectors,
        patch_embed_weight,
        decoded,
        decoder_weight,
        velocity_t,
        normed,
        adapter_up,
        lowrank_t,
        heads,
    )
    own_scores = scores_wide[:, 0].astype(jnp.bfloat16)
    grad_b = jnp.concatenate([grad_b[:, :half], grad_b[:, half:]], 0)
    lead, front = group == 0, mp == 0
    grad_a = jnp.concatenate(
        [jnp.where(front, grad_kept, grad_taken), jnp.where(front, grad_taken, grad_kept)], 0
    )
    mine = jnp.where(lead, grad_a, grad_b)
    given_part = jnp.where(lead, grad_b, grad_a).astype(jnp.bfloat16)
    mine = mine + swap_cores(given_part).astype(jnp.float32)
    total = add_over_chips(mine)
    passed = swap_cores(total)
    total_a = jnp.where(lead, total, passed)
    total_b = jnp.where(lead, passed, total)
    rank = adapter_up.shape[0]
    grad_a = lax.dynamic_slice_in_dim(total_a, mp * rank, rank, 0).astype(jnp.float32).T
    grad_b = jnp.concatenate([total_b[:rank], total_b[rank:]], 1).astype(jnp.float32)
    return (grad_a, grad_b, own_scores)


def solution(mesh):
    fine = Mesh(mesh.devices.reshape(2, 4, 2, 8, 2), ("group", "x", "yl", "z", "mp"))
    dp = ("x", "yl", "z")
    rows = ("group",) + dp
    return jax.shard_map(
        shards,
        mesh=fine,
        in_specs=(
            P(rows, "mp"),
            P(rows + ("mp",), None),
            P("mp", dp),
            P("mp", None),
            P(),
            P(),
            P(),
            P(),
            P(),
            P(),
            P(rows + ("mp",), None),
            P(),
            P(),
            P(),
            P(),
            P(dp, None, None),
            P(rows + ("mp",), None),
            P(rows + ("mp",), None),
        ),
        out_specs=(P("mp", None), P(), P(rows + ("mp",))),
        check_vma=False,
    )
```
